256 devices in a mesh: adapter: 32 (over x, y, core), tensor: 8 (over z).
Axes of the slice: x: 4, y: 4, z: 8, core: 2. Of those that a mesh axis runs over, the one named last changes fastest.
Arguments:
- activations: bfloat16 [49152, 8192], P('adapter', 'tensor'), may hold values from -6 to 6
- output_gradient: bfloat16 [49152, 1024], P('adapter', 'tensor'), may hold values from -1.5 to 1.5
- adapter_of_row: int32 [49152, 1], P('adapter'), may hold values from 0 to 127; in each aligned block of 1536 rows (0 to 1535, 1536 to 3071, ...) at most 15 rows name the same one
- frozen_value_weight: bfloat16 [8192, 1024], P('tensor'), may hold values from -0.1875 to 0.1875
- adapter_down_weight: bfloat16 [128, 64, 8192], P('adapter', None, 'tensor'), may hold values from -0.0625 to 0.0625
- adapter_up_weight: bfloat16 [128, 64, 1024], P('adapter', None, 'tensor'), may hold values from -0.1875 to 0.1875
Outputs:
- input_gradient: bfloat16 [49152, 8192], P('adapter', 'tensor')
- down_gradient: float32 [128, 64, 8192], P('adapter', None, 'tensor')
- up_gradient: float32 [128, 64, 1024], P('adapter', None, 'tensor')
The draws below stay inside these ranges and needn't reach their ends.
Inputs may be any that keep to these rules, and one draw needn't show every extreme that they name: `adapter_of_row`: among the rows of one device no adapter id appears more than 15 times, and in every draw some adapter appears exactly 15 times among some device's rows. Every adapter appears somewhere.
All inputs are finite; a program needn't handle non-finite values.
Results may differ from the reference program's by a relative error of at most 0.0034.
Values may be sent and summed in bfloat16 or wider, within the bound.
A program may use at most 128 MiB of HBM per device.

```python
import math
import jax
import jax.numpy as jnp
import numpy as np
from jax import lax

MODEL_WIDTH = 8192
VALUE_WIDTH = 1024
ADAPTER_RANK = 64
TOK_DEV = 1536
ADAPTER_TOTAL = 128
TOKENS = 49152
MOST = 15
N_ADAPTER = 32


def steps_of(own_key, extent, cuts, smallest, top_value):
    def one(dim, shards_of):
        steps = jax.random.uniform(jax.random.fold_in(jax.random.fold_in(own_key, 6), dim), (shards_of,), jnp.float32, smallest / len(cuts), top_value / len(cuts))
        return jnp.repeat(jnp.exp(steps), extent[dim] // shards_of).reshape((-1,) + (1,) * (len(extent) - dim - 1))

    level = one(*cuts[0])
    for cut in cuts[1:]:
        level = level * one(*cut)
    return level


def shared_out(stream_key, own, number, rows, number_of, top, most, lean):
    sequence = jax.random.permutation(stream_key, number_of)
    packed, ordinary = portions_of(number_of, rows * top, most, lean, True), portions_of(number_of, rows * top, most, lean, False)
    places = jnp.arange(number_of)

    def named(sizes, turn):
        used = int((sizes > 0).sum())
        fixed = max(1, used // 4)
        shifted = fixed + (places - fixed + turn * (used - fixed)) % max(1, number_of - fixed)
        return jnp.zeros((number_of,), jnp.int32).at[sequence[jnp.where(places < fixed, places, shifted)]].set(jnp.asarray(sizes, jnp.int32))

    sizes = jnp.where(number % 4 == 0, named(packed, number // 4), named(ordinary, number - number // 4 - 1))
    mixed = jax.random.permutation(jax.random.fold_in(own, 3), number_of)
    donor, receiver = mixed[0:number_of // 2 * 2:2], mixed[1:number_of // 2 * 2:2]
    slack = jnp.minimum(sizes[donor] - 1, most - sizes[receiver]) // 2
    slack = jnp.where((donor == sequence[0]) | (receiver == sequence[0]) | (sizes[receiver] == 0), 0, jnp.maximum(slack, 0))
    shifted = jax.random.randint(jax.random.fold_in(own, 4), (number_of // 2,), 0, 1 << 20) % (slack + 1)
    sizes = sizes.at[donor].add(-shifted).at[receiver].add(shifted)
    members = jnp.searchsorted(jnp.cumsum(sizes), jnp.arange(rows * top), side="right").astype(jnp.int32)
    table = members.reshape(top, rows).T
    table = table[jax.random.permutation(jax.random.fold_in(own, 1), rows)]
    turn = jax.random.randint(jax.random.fold_in(own, 2), (rows, 1), 0, top)
    return jnp.take_along_axis(table, (jnp.arange(top)[None, :] + turn) % top, axis=1)


def portions_of(amount, total, reach, skew, full):
    weights = [(1 << 20) // math.isqrt(rank ** skew) + 1 for rank in range(1, amount + 1)]
    largest = reach if full else min(reach, max(-(-total // amount), total * weights[0] // sum(weights)))
    least = 1 if total - largest >= amount - 1 else 0
    counts, rest = [largest] + [least] * (amount - 1), total - largest - least * (amount - 1)
    while rest > 0:
        candidates = [i for i in range(1, amount) if counts[i] < largest] or [i for i in range(1, amount) if counts[i] < reach]
        mass, budget = sum([weights[i] for i in candidates]), rest
        for i in candidates:
            more = min(reach - counts[i], max(1, budget * weights[i] // mass), rest)
            counts[i] = counts[i] + more
            rest = rest - more
    return np.array(counts)


def bell_draw(rng, shape, spread, most, shards=(), held_as=jnp.bfloat16):
    loudness = steps_of(rng, shape, shards, -0.22, 0.18) if shards else 1.0
    values = jax.random.normal(rng, shape, jnp.float32) * spread * loudness
    return jnp.minimum(jnp.maximum(values, -most), most).astype(held_as)


def setup_inputs(seed: int = 0) -> dict:
    streams_of = jax.random.split(jax.random.key(seed), 7)
    activations = bell_draw(streams_of[0], (TOKENS, MODEL_WIDTH), 1.0, 6.0, ((0, 32), (1, 8)))
    output_gradient = bell_draw(streams_of[1], (TOKENS, VALUE_WIDTH), 0.25, 1.5, ((0, 32), (1, 8)))
    adapter_of_row_keys = jax.random.split(jax.random.fold_in(streams_of[2], 1), TOKENS // TOK_DEV)
    adapter_of_row_turns = jax.random.permutation(jax.random.fold_in(streams_of[2], 3), TOKENS // TOK_DEV)
    adapter_of_row = jax.vmap(lambda own, number: shared_out(jax.random.fold_in(streams_of[2], 2), own, number, TOK_DEV, ADAPTER_TOTAL, 1, MOST, 2))(adapter_of_row_keys, adapter_of_row_turns).reshape((TOKENS, 1))
    frozen_value_weight = bell_draw(streams_of[3], (MODEL_WIDTH, VALUE_WIDTH), VALUE_WIDTH ** -0.5, 0.1875, ((0, 8),))
    adapter_down_weight = bell_draw(streams_of[4], (ADAPTER_TOTAL, ADAPTER_RANK, MODEL_WIDTH), MODEL_WIDTH ** -0.5, 0.0625, ((0, 32), (2, 8)))
    adapter_up_weight = bell_draw(streams_of[5], (ADAPTER_TOTAL, ADAPTER_RANK, VALUE_WIDTH), VALUE_WIDTH ** -0.5, 0.1875, ((0, 32), (2, 8)))
    return dict(activations=activations, output_gradient=output_gradient, adapter_of_row=adapter_of_row, frozen_value_weight=frozen_value_weight, adapter_down_weight=adapter_down_weight, adapter_up_weight=adapter_up_weight)


adapter_scale = 2.0


def reference(activations, output_gradient, adapter_of_row, frozen_value_weight, adapter_down_weight, adapter_up_weight):
    token_count = activations.shape[0]
    capacity = N_ADAPTER * MOST
    token_ids = adapter_of_row[:, 0].astype(jnp.int32)
    padded_x = jnp.concatenate([activations, jnp.zeros((1, MODEL_WIDTH), activations.dtype)], axis=0)
    padded_g = jnp.concatenate([output_gradient, jnp.zeros((1, VALUE_WIDTH), output_gradient.dtype)], axis=0)

    def single_adapter(adapter_rows, adapter_number):
        token_row_index = jnp.nonzero(token_ids == adapter_number, size=capacity, fill_value=token_count)[0].astype(jnp.int32)
        activation_rows = padded_x[token_row_index]
        gradient_rows = padded_g[token_row_index]
        down_matrix = adapter_down_weight[adapter_number]
        up_matrix = adapter_up_weight[adapter_number]
        rank_value = jnp.dot(activation_rows, down_matrix.T, preferred_element_type=jnp.float32).astype(jnp.bfloat16)
        value_backward = jnp.dot(gradient_rows, up_matrix.T, preferred_element_type=jnp.float32).astype(jnp.bfloat16)
        down_gradient_local = adapter_scale * jnp.dot(value_backward.T, activation_rows, preferred_element_type=jnp.float32)
        up_gradient_local = adapter_scale * jnp.dot(rank_value.T, gradient_rows, preferred_element_type=jnp.float32)
        adapter_share = (adapter_scale * jnp.dot(value_backward, down_matrix, preferred_element_type=jnp.float32)).astype(jnp.bfloat16)
        adapter_rows = adapter_rows.at[token_row_index].set(adapter_share)
        return adapter_rows, (down_gradient_local, up_gradient_local)

    starting_carry = jnp.zeros((token_count + 1, MODEL_WIDTH), jnp.bfloat16)
    adapter_stack, (down_gradient, up_gradient) = lax.scan(single_adapter, starting_carry, jnp.arange(ADAPTER_TOTAL, dtype=jnp.int32))
    frozen_share = jnp.dot(output_gradient, frozen_value_weight.T, preferred_element_type=jnp.float32)
    input_gradient = (frozen_share + adapter_stack[:token_count].astype(jnp.float32)).astype(jnp.bfloat16)
    return input_gradient, down_gradient, up_gradient
```

```python
import jax
import jax.numpy as jnp
from jax import lax
from jax.experimental import pallas as pl
from jax.experimental.pallas import tpu as pltpu
from jax.sharding import PartitionSpec as P

adapter_scale = 2.0
MESH = pl.DeviceIdType.MESH
BF = jnp.bfloat16
F32 = jnp.float32

MOST = 15
SLOTS = 240
HALF = 512
ROWS = 1536
RANK = 64
GW = 128
OWN = 256

(U_A, U_B, G_A, G_B, D_A, D_B, X_A, X_B, B_RS, B_AG, L_RS, L_AG, R_A, R_B, DG_A, DG_B, UG_A, UG_B) = range(18)


def rank_kernel(
    x_ref, g_ref, sa_ref, sb_ref, d_ref, u_ref,
    reta_ref, retb_ref, down_ref, up_ref,
    sxa, sxb, sga, sgb, rxa, rxb, rga, rgb,
    da, db, ua, ub,
    maskf, maskb,
    bpart, bz, bsum, ball, lpart, lz, lsum, lall,
    ma, mb, outa, outb,
    dga, dgb, dgra, dgrb, dgo, uga, ugb, ugra, ugrb, ugo,
    ss, rs, loc,
):
    a = lax.axis_index("adapter")
    z = lax.axis_index("tensor")
    c = a % 2
    y = (a // 2) % 4
    x = a // 8
    m_a = y * 2 + c
    m_b = x * 2 + c

    def on_a(t):
        return ((x * 4 + t // 2) * 2 + t % 2, z)

    def on_b(t):
        return (((t // 2) * 4 + y) * 2 + t % 2, z)

    def ring_x(t):
        return ((t * 4 + y) * 2 + c, z)

    def ring_y(t):
        return ((x * 4 + t) * 2 + c, z)

    def ring_z(t):
        return (a, t)

    def copy(kind, src, dst, to, me, device):
        return pltpu.make_async_remote_copy(
            src_ref=src, dst_ref=dst, send_sem=ss.at[kind, to], recv_sem=rs.at[kind, me],
            device_id=device, device_id_type=MESH,
        )

    def arrived(kind, dst, frm):
        pltpu.make_async_remote_copy(
            src_ref=dst, dst_ref=dst, send_sem=ss.at[kind, frm], recv_sem=rs.at[kind, frm],
            device_id=(a, z), device_id_type=MESH,
        ).wait_recv()

    def left(kind, src, to):
        pltpu.make_async_remote_copy(
            src_ref=src, dst_ref=src, send_sem=ss.at[kind, to], recv_sem=rs.at[kind, to],
            device_id=(a, z), device_id_type=MESH,
        ).wait_send()

    barrier = pltpu.get_barrier_semaphore()

    @pl.loop(1, 8)
    def _(d):
        pl.semaphore_signal(barrier, inc=1, device_id=on_a((m_a + d) % 8), device_id_type=MESH)
        pl.semaphore_signal(barrier, inc=1, device_id=ring_z((z + d) % 8), device_id_type=MESH)

    @pl.loop(2, 8)
    def _(d):
        t = ((x * 2) + d) % 8
        pl.semaphore_signal(barrier, inc=1, device_id=on_b(t), device_id_type=MESH)

    pl.semaphore_wait(barrier, 20)

    @pl.loop(1, 4)
    def _(d):
        tx = (x + d) % 4
        ty = (y + d) % 4
        copy(U_A, u_ref, ua.at[x], tx, x, ring_x(tx)).start()
        copy(U_B, u_ref, ub.at[y], ty, y, ring_y(ty)).start()

    ua[x] = u_ref[...]
    ub[y] = u_ref[...]

    slot_rows = lax.broadcasted_iota(jnp.int32, (SLOTS, ROWS), 0)

    def choose(s_ref, t):
        return jnp.where(slot_rows + t * SLOTS == s_ref[...], 1.0, 0.0).astype(BF)

    def route(kind, m, on, s_ref, value, send, recv, d):
        t = (m + d) % 8
        block = jnp.dot(choose(s_ref, t), value, preferred_element_type=F32).astype(BF)

        @pl.when(d == 0)
        def _():
            recv[m] = block

        @pl.when(d != 0)
        def _():
            send[t] = block
            copy(kind, send.at[t], recv.at[m], t, m, on(t)).start()

    def near_first(k):
        return jnp.where(k < 4, 2 + 4 * (k % 2) + k // 2, 4 * (1 - (k - 4) // 2) + k % 2)

    @pl.loop(0, 8)
    def _(k):
        d = near_first(k)
        route(G_A, m_a, on_a, sa_ref, g_ref[...], sga, rga, d)
        route(G_B, m_b, on_b, sb_ref, g_ref[...], sgb, rgb, d)

    @pl.loop(1, 4)
    def _(d):
        tx = (x + d) % 4
        ty = (y + d) % 4
        copy(D_A, d_ref.at[:, pl.ds(0, HALF)], da.at[x], tx, x, ring_x(tx)).start()
        copy(D_B, d_ref.at[:, pl.ds(HALF, HALF)], db.at[y], ty, y, ring_y(ty)).start()

    da[x] = d_ref[:, :HALF]
    db[y] = d_ref[:, HALF:]

    @pl.loop(0, 8)
    def _(k):
        d = near_first(k)
        route(X_A, m_a, on_a, sa_ref, x_ref[:, :HALF], sxa, rxa, d)
        route(X_B, m_b, on_b, sb_ref, x_ref[:, HALF:], sxb, rxb, d)

    first = (lax.broadcasted_iota(jnp.int32, (SLOTS, 1024), 1) >> 6) * MOST
    row = lax.broadcasted_iota(jnp.int32, (SLOTS, 1024), 0)
    mask = jnp.where((row >= first) & (row < first + MOST), 1.0, 0.0)
    maskf[...] = mask
    maskb[...] = mask.astype(BF)
    low_lanes = lax.broadcasted_iota(jnp.int32, (SLOTS, 128), 1) < RANK

    def fold(rows, weights):
        product = lax.dot_general(rows, weights, (((1,), (1,)), ((), ())), preferred_element_type=F32)
        product = product * maskf[...]
        total = product[:, :128]
        for i in range(1, 8):
            total = total + product[:, i * 128 : (i + 1) * 128]
        return total + pltpu.roll(total, RANK, 1)

    def pair(rows_a, weights_a, rows_b, weights_b):
        return jnp.where(low_lanes, fold(rows_a, weights_a), fold(rows_b, weights_b))

    def spread(both, is_a):
        wide = both.astype(F32)
        turned = pltpu.roll(wide, RANK, 1)
        one = (jnp.where(low_lanes, wide, turned) if is_a else jnp.where(low_lanes, turned, wide)).astype(BF)
        return jnp.concatenate([one] * 8, axis=1) * maskb[...]

    @pl.loop(1, 4)
    def _(d):
        fx = (x + d) % 4
        fy = (y + d) % 4
        arrived(U_A, ua.at[fx], fx)
        arrived(U_B, ub.at[fy], fy)

    @pl.loop(1, 8)
    def _(d):
        fa = (m_a + d) % 8
        fb = (m_b + d) % 8
        arrived(G_A, rga.at[fa], fa)
        arrived(G_B, rgb.at[fb], fb)

    def partial_sums(kind, part, held, k, rows_a, weights_a, rows_b, weights_b):
        t = (z + k) % 8
        value = pair(rows_a[t], weights_a[...].reshape(1024, -1), rows_b[t], weights_b[...].reshape(1024, -1))

        @pl.when(k == 0)
        def _():
            held[z] = value

        @pl.when(k != 0)
        def _():
            part[t] = value
            copy(kind, part.at[t], held.at[z], t, z, ring_z(t)).start()

    @pl.loop(0, 8)
    def _(k):
        partial_sums(B_RS, bpart, bz, k, rga, ua, rgb, ub)

    @pl.loop(1, 4)
    def _(d):
        fx = (x + d) % 4
        fy = (y + d) % 4
        arrived(D_A, da.at[fx], fx)
        arrived(D_B, db.at[fy], fy)

    @pl.loop(1, 8)
    def _(d):
        fa = (m_a + d) % 8
        fb = (m_b + d) % 8
        arrived(X_A, rxa.at[fa], fa)
        arrived(X_B, rxb.at[fb], fb)

    def finish_sums(rs_kind, ag_kind, held, total, everything):
        @pl.loop(1, 8)
        def _(d):
            t = (z + d) % 8
            arrived(rs_kind, held.at[t], t)

        acc = held[0]
        for i in range(1, 8):
            acc = acc + held[i]
        total[...] = acc.astype(BF)
        everything[z] = acc.astype(BF)

        @pl.loop(1, 8)
        def _(d):
            t = (z + d) % 8
            copy(ag_kind, total, everything.at[z], t, z, ring_z(t)).start()

    finish_sums(B_RS, B_AG, bz, bsum, ball)

    @pl.loop(0, 8)
    def _(k):
        partial_sums(L_RS, lpart, lz, k, rxa, da, rxb, db)

    @pl.loop(1, 8)
    def _(d):
        t = (z + d) % 8
        arrived(B_AG, ball.at[t], t)

    def give_back(kind, m, on, masked, is_a, weights, out, ret, d):
        s = (m + d) % 8
        block = spread(ball[s], is_a)
        masked[s] = block
        out[s] = (
            adapter_scale * jnp.dot(block, weights[...].reshape(1024, HALF), preferred_element_type=F32)
        ).astype(BF)

        @pl.when(d != 0)
        def _():
            copy(kind, out.at[s], ret.at[m], s, m, on(s)).start()

        @pl.when(d == 0)
        def _():
            pltpu.make_async_copy(out.at[s], ret.at[m], loc.at[kind - R_A]).start()

    @pl.loop(0, 8)
    def _(k):
        d = near_first(k)
        give_back(R_A, m_a, on_a, ma, True, da, outa, reta_ref, d)
        give_back(R_B, m_b, on_b, mb, False, db, outb, retb_ref, d)

    def gradient(masked, rows, q):
        return adapter_scale * lax.dot_general(
            masked[:, :, pl.ds(pl.multiple_of(q * OWN, OWN), OWN)].reshape(8 * SLOTS, OWN),
            rows[...].reshape(8 * SLOTS, -1),
            (((0,), (0,)), ((), ())),
            preferred_element_type=F32,
        )

    def to_owner(kind, m, ring, masked, rows, part, recv, own, half, d):
        q = (m + d) % 4
        value = gradient(masked, rows, q)

        @pl.when(d == 4)
        def _():
            own[half] = value

        @pl.when(d != 4)
        def _():
            part[q] = value.astype(part.dtype)
            copy(kind, part.at[q], recv.at[m], q, m, ring(q)).start()

    @pl.loop(1, 5)
    def _(d):
        to_owner(DG_A, x, ring_x, ma, rxa, dga, dgra, dgo, 0, d)
        to_owner(DG_B, y, ring_y, mb, rxb, dgb, dgrb, dgo, 1, d)

    finish_sums(L_RS, L_AG, lz, lsum, lall)

    @pl.loop(1, 8)
    def _(d):
        t = (z + d) % 8
        arrived(L_AG, lall.at[t], t)

    @pl.loop(0, 8)
    def _(s):
        ma[s] = spread(lall[s], True)
        mb[s] = spread(lall[s], False)

    @pl.loop(1, 5)
    def _(d):
        to_owner(UG_A, x, ring_x, ma, rga, uga, ugra, ugo, 0, d)
        to_owner(UG_B, y, ring_y, mb, rgb, ugb, ugrb, ugo, 1, d)

    @pl.loop(1, 4)
    def _(d):
        fx = (x + d) % 4
        fy = (y + d) % 4
        arrived(DG_A, dgra.at[fx], fx)
        arrived(DG_B, dgrb.at[fy], fy)
        dgo[0] += dgra[fx].astype(F32)
        dgo[1] += dgrb[fy].astype(F32)

    down_ref[:, :HALF] = dgo[0]
    down_ref[:, HALF:] = dgo[1]

    @pl.loop(1, 4)
    def _(d):
        fx = (x + d) % 4
        fy = (y + d) % 4
        arrived(UG_A, ugra.at[fx], fx)
        arrived(UG_B, ugrb.at[fy], fy)
        ugo[0] += ugra[fx]
        ugo[1] += ugrb[fy]

    up_ref[...] = ugo[0] + ugo[1]

    @pl.loop(1, 8)
    def _(d):
        ta = (m_a + d) % 8
        tb = (m_b + d) % 8
        tz = (z + d) % 8
        arrived(R_A, reta_ref.at[ta], ta)
        arrived(R_B, retb_ref.at[tb], tb)
        left(G_A, sga.at[ta], ta)
        left(G_B, sgb.at[tb], tb)
        left(X_A, sxa.at[ta], ta)
        left(X_B, sxb.at[tb], tb)
        left(R_A, outa.at[ta], ta)
        left(R_B, outb.at[tb], tb)
        left(B_RS, bpart.at[tz], tz)
        left(L_RS, lpart.at[tz], tz)
        left(B_AG, bsum, tz)
        left(L_AG, lsum, tz)

    @pl.loop(1, 4)
    def _(d):
        tx = (x + d) % 4
        ty = (y + d) % 4
        left(U_A, u_ref, tx)
        left(U_B, u_ref, ty)
        left(D_A, d_ref.at[:, pl.ds(0, HALF)], tx)
        left(D_B, d_ref.at[:, pl.ds(HALF, HALF)], ty)
        left(DG_A, dga.at[tx], tx)
        left(DG_B, dgb.at[ty], ty)
        left(UG_A, uga.at[tx], tx)
        left(UG_B, ugb.at[ty], ty)

    pltpu.make_async_copy(outa.at[m_a], reta_ref.at[m_a], loc.at[0]).wait()
    pltpu.make_async_copy(outb.at[m_b], retb_ref.at[m_b], loc.at[1]).wait()


def rank_part(x, g, slot_a, slot_b, d, u):
    vmem = pl.BlockSpec(memory_space=pltpu.VMEM)
    hbm = pl.BlockSpec(memory_space=pl.ANY)
    block = lambda width, dtype=BF: pltpu.VMEM((8, SLOTS, width), dtype)
    chunk = lambda width, dtype=BF: pltpu.VMEM((4, OWN, width), dtype)
    return pl.pallas_call(
        rank_kernel,
        out_shape=(
            jax.ShapeDtypeStruct((8, SLOTS, HALF), BF),
            jax.ShapeDtypeStruct((8, SLOTS, HALF), BF),
            jax.ShapeDtypeStruct((OWN, 2 * HALF), F32),
            jax.ShapeDtypeStruct((OWN, GW), F32),
        ),
        in_specs=[vmem] * 6,
        out_specs=(hbm, hbm, vmem, vmem),
        scratch_shapes=[
            block(HALF), block(HALF), block(GW), block(GW),
            block(HALF), block(HALF), block(GW), block(GW),
            chunk(HALF), chunk(HALF), chunk(GW), chunk(GW),
            pltpu.VMEM((SLOTS, 1024), F32), pltpu.VMEM((SLOTS, 1024), BF),
            block(128, F32), block(128, F32), pltpu.VMEM((SLOTS, 128), BF), block(128),
            block(128, F32), block(128, F32), pltpu.VMEM((SLOTS, 128), BF), block(128),
            block(1024), block(1024), block(HALF), block(HALF),
            chunk(HALF), chunk(HALF), chunk(HALF), chunk(HALF), pltpu.VMEM((2, OWN, HALF), F32),
            chunk(GW, F32), chunk(GW, F32), chunk(GW, F32), chunk(GW, F32), pltpu.VMEM((2, OWN, GW), F32),
            pltpu.SemaphoreType.DMA((18, 8)), pltpu.SemaphoreType.DMA((18, 8)), pltpu.SemaphoreType.DMA((2,)),
        ],
        compiler_params=pltpu.CompilerParams(
            collective_id=0, has_side_effects=True, vmem_limit_bytes=60 * 2**20
        ),
        cost_estimate=pl.CostEstimate(flops=30 * 10**9, bytes_accessed=20 * 10**6, transcendentals=0),
        name="rank_part",
    )(x, g, slot_a, slot_b, d, u)


def join_kernel(g_ref, w_ref, sa_ref, sb_ref, ra_ref, rb_ref, out_ref):
    rows = g_ref.shape[0]
    slots = lax.broadcasted_iota(jnp.int32, (rows, 8 * SLOTS), 1)
    for half, (s_ref, r_ref) in enumerate(((sa_ref, ra_ref), (sb_ref, rb_ref))):
        base = lax.dot_general(
            g_ref[...], w_ref[half * HALF : (half + 1) * HALF, :], (((1,), (1,)), ((), ())),
            preferred_element_type=F32,
        )
        pick = jnp.where(slots == s_ref[...], 1.0, 0.0).astype(BF)
        base = base + jnp.dot(pick, r_ref[...].reshape(8 * SLOTS, HALF), preferred_element_type=F32)
        out_ref[:, half * HALF : (half + 1) * HALF] = base.astype(BF)


def join(g_full, w, slot_a, slot_b, ret_a, ret_b):
    rows = 256
    whole = lambda shape: pl.BlockSpec(shape, lambda i: (0,) * len(shape))
    part = lambda width: pl.BlockSpec((rows, width), lambda i: (i, 0))
    return pl.pallas_call(
        join_kernel,
        grid=(ROWS // rows,),
        out_shape=jax.ShapeDtypeStruct((ROWS, 2 * HALF), BF),
        in_specs=[
            part(1024), whole((1024, 1024)), part(1), part(1),
            whole((8, SLOTS, HALF)), whole((8, SLOTS, HALF)),
        ],
        out_specs=part(2 * HALF),
        compiler_params=pltpu.CompilerParams(vmem_limit_bytes=48 * 2**20),
        name="join",
    )(g_full, w, slot_a, slot_b, ret_a, ret_b)


def body(
    activations,
    output_gradient,
    adapter_of_row,
    frozen_value_weight,
    adapter_down_weight,
    adapter_up_weight,
):
    ids = adapter_of_row[:, 0]
    onehot = (ids[:, None] == jnp.arange(128, dtype=jnp.int32)[None, :]).astype(jnp.int32)
    position = jnp.sum(jnp.cumsum(onehot, axis=0) * onehot, axis=1) - 1
    owner, within = ids // 4, ids % 4
    core, y, x = owner % 2, (owner // 2) % 4, owner // 8
    slot_a = (y * 2 + core) * SLOTS + (x * 4 + within) * MOST + position
    slot_b = (x * 2 + core) * SLOTS + (y * 4 + within) * MOST + position
    g_full = lax.all_gather(output_gradient, "tensor", axis=1, tiled=True)
    ret_a, ret_b, down, up = rank_part(
        activations,
        output_gradient,
        slot_a[None, :],
        slot_b[None, :],
        adapter_down_weight.reshape(OWN, 2 * HALF),
        adapter_up_weight.reshape(OWN, GW),
    )
    input_gradient = join(
        g_full, frozen_value_weight, slot_a[:, None], slot_b[:, None], ret_a, ret_b
    )
    return input_gradient, down.reshape(4, RANK, 2 * HALF), up.reshape(4, RANK, GW)


def solution(mesh):
    in_specs = (
        P("adapter", "tensor"),
        P("adapter", "tensor"),
        P("adapter", None),
        P("tensor", None),
        P("adapter", None, "tensor"),
        P("adapter", None, "tensor"),
    )
    out_specs = (P("adapter", "tensor"), P("adapter", None, "tensor"), P("adapter", None, "tensor"))
    return jax.shard_map(body, mesh=mesh, in_specs=in_specs, out_specs=out_specs, check_vma=False)
```

```python
import jax
import jax.numpy as jnp
from jax import lax
from jax.experimental import pallas as pl
from jax.experimental.pallas import tpu as pltpu
from jax.sharding import PartitionSpec as P

adapter_scale = 2.0
MESH = pl.DeviceIdType.MESH
BF = jnp.bfloat16
F32 = jnp.float32

MOST = 15
SLOTS = 240
HALF = 512
ROWS = 1536
RANK = 64
GW = 128
OWN = 256
TILE = 256

(U_A, U_B, G_A, G_B, D_A, D_B, X_A, X_B, R_A, R_B, DG_A, DG_B, UG_A, UG_B, GR, GL,
 B_RELAY, B_FINAL, B_NEAR, B_FAR, L_RELAY, L_FINAL, L_NEAR, L_FAR) = range(24)


def adapter_kernel(
    ids_ref, x_hbm, g_ref, w_hbm, d_ref, u_ref,
    out_hbm, down_ref, up_ref,
    xv, wv, sa_ref, sb_ref, cols,
    sxa, sxb, sga, sgb, rxa, rxb, rga, rgb,
    da, db, ua, ub, maskb,
    bpart, brelay, bfinal, ball, lpart, lrelay, lfinal, lall,
    ma, mb, reta, retb,
    dga, dgb, dgra, dgrb, dgo, uga, ugb, ugra, ugrb, ugo,
    gfull, acc,
    ss, rs, loc,
):
    a = lax.axis_index("adapter")
    z = lax.axis_index("tensor")
    c = a % 2
    y = (a // 2) % 4
    x = a // 8
    m_a = y * 2 + c
    m_b = x * 2 + c
    side = 2 * (z % 2) - 1

    def on_a(t):
        return ((x * 4 + t // 2) * 2 + t % 2, z)

    def on_b(t):
        return (((t // 2) * 4 + y) * 2 + t % 2, z)

    def ring_x(t):
        return ((t * 4 + y) * 2 + c, z)

    def ring_y(t):
        return ((x * 4 + t) * 2 + c, z)

    def zz(i):
        return (z + i + 16) % 8

    def on_z(i):
        return (a, zz(i))

    def copy(kind, src, dst, to, me, device):
        return pltpu.make_async_remote_copy(
            src_ref=src, dst_ref=dst, send_sem=ss.at[kind, to], recv_sem=rs.at[kind, me],
            device_id=device, device_id_type=MESH,
        )

    def arrived(kind, dst, frm):
        copy(kind, dst, dst, frm, frm, (a, z)).wait_recv()

    def left(kind, src, to):
        copy(kind, src, src, to, to, (a, z)).wait_send()

    def near_first(k):
        return jnp.where(k < 4, 2 + 4 * (k % 2) + k // 2, 4 * (1 - (k - 4) // 2) + k % 2)

    x_in = pltpu.make_async_copy(x_hbm, xv, loc.at[0])
    x_in.start()
    w_in = pltpu.make_async_copy(w_hbm, wv, loc.at[1])
    w_in.start()

    barrier = pltpu.get_barrier_semaphore()

    @pl.loop(1, 8)
    def _(d):
        pl.semaphore_signal(barrier, inc=1, device_id=on_a((m_a + d) % 8), device_id_type=MESH)
        pl.semaphore_signal(barrier, inc=1, device_id=on_z(d), device_id_type=MESH)

    @pl.loop(2, 8)
    def _(d):
        t = ((x * 2) + d) % 8
        pl.semaphore_signal(barrier, inc=1, device_id=on_b(t), device_id_type=MESH)

    with jax.named_scope("slots"):
        ids = ids_ref[...]
        hot = jnp.where(lax.broadcasted_iota(jnp.int32, (128, ROWS), 0) == ids, 1.0, 0.0)
        before = jnp.where(
            lax.broadcasted_iota(jnp.int32, (TILE, TILE), 0) < lax.broadcasted_iota(jnp.int32, (TILE, TILE), 1), 1.0, 0.0
        ).astype(BF)
        seen = jnp.zeros((128, 1), F32)
        places = []
        for q in range(ROWS // TILE):
            part = hot[:, q * TILE : (q + 1) * TILE]
            count = jnp.dot(part.astype(BF), before, preferred_element_type=F32) + seen
            places.append(jnp.sum(count * part, axis=0, keepdims=True))
            seen = seen + jnp.sum(part, axis=1, keepdims=True)
        place = jnp.concatenate(places, axis=1).astype(jnp.int32)
        owner, within = ids >> 2, ids & 3
        core, oy, ox = owner & 1, (owner >> 1) & 3, owner >> 3
        slot_a = (oy * 2 + core) * SLOTS + (ox * 4 + within) * MOST + place
        slot_b = (ox * 2 + core) * SLOTS + (oy * 4 + within) * MOST + place
        sa_ref[...] = slot_a
        sb_ref[...] = slot_b
        cols[...] = jnp.concatenate([slot_a.astype(F32), slot_b.astype(F32)] * 4, axis=0).T

        first = (lax.broadcasted_iota(jnp.int32, (SLOTS, 1024), 1) >> 6) * MOST
        row = lax.broadcasted_iota(jnp.int32, (SLOTS, 1024), 0)
        maskb[...] = jnp.where((row >= first) & (row < first + MOST), 1.0, 0.0).astype(BF)

    pl.semaphore_wait(barrier, 20)

    @pl.loop(1, 4)
    def _(d):
        tx = (x + d) % 4
        ty = (y + d) % 4
        copy(U_A, u_ref, ua.at[x], tx, x, ring_x(tx)).start()
        copy(U_B, u_ref, ub.at[y], ty, y, ring_y(ty)).start()

    ua[x] = u_ref[...]
    ub[y] = u_ref[...]

    def g_cols(i):
        return pl.ds(pl.multiple_of(zz(i) * GW, GW), GW)

    def g_whole(i):
        return gfull.at[:, g_cols(i)]

    def g_half(i, upper):
        return gfull.at[pl.ds(upper * (ROWS // 2), ROWS // 2), g_cols(i)]

    copy(GR, g_ref, g_whole(0), 0, 1, on_z(1)).start()
    copy(GL, g_ref, g_whole(0), 0, 1, on_z(-1)).start()

    def g_step(i):
        arrived(GR, g_whole(-i), i)
        arrived(GL, g_whole(i), i)
        if i < 3:
            copy(GR, g_whole(-i), g_whole(-i), i, i + 1, on_z(1)).start()
            copy(GL, g_whole(i), g_whole(i), i, i + 1, on_z(-1)).start()
        else:
            copy(GR, g_half(-i, 0), g_half(-i, 0), i, i + 1, on_z(1)).start()
            copy(GL, g_half(i, 1), g_half(i, 1), i, i + 1, on_z(-1)).start()

    slot_rows = lax.broadcasted_iota(jnp.int32, (SLOTS, ROWS), 0)

    def choose(s_ref, t):
        return jnp.where(slot_rows + t * SLOTS == s_ref[...], 1.0, 0.0).astype(BF)

    def route(kind, m, on, s_ref, value, send, recv, d):
        t = (m + d) % 8
        block = jnp.dot(choose(s_ref, t), value, preferred_element_type=F32).astype(BF)

        @pl.when(d == 0)
        def _():
            recv[m] = block

        @pl.when(d != 0)
        def _():
            send[t] = block
            copy(kind, send.at[t], recv.at[m], t, m, on(t)).start()

    with jax.named_scope("route_g"):

        @pl.loop(0, 8)
        def _(k):
            d = near_first(k)
            route(G_A, m_a, on_a, sa_ref, g_ref[...], sga, rga, d)
            route(G_B, m_b, on_b, sb_ref, g_ref[...], sgb, rgb, d)

    gfull[:, g_cols(0)] = g_ref[...]

    @pl.loop(1, 4)
    def _(d):
        tx = (x + d) % 4
        ty = (y + d) % 4
        copy(D_A, d_ref.at[:, pl.ds(0, HALF)], da.at[x], tx, x, ring_x(tx)).start()
        copy(D_B, d_ref.at[:, pl.ds(HALF, HALF)], db.at[y], ty, y, ring_y(ty)).start()

    da[x] = d_ref[:, :HALF]
    db[y] = d_ref[:, HALF:]
    x_in.wait()

    def route_x(lo, hi):
        with jax.named_scope("route_x"):

            @pl.loop(lo, hi)
            def _(k):
                d = near_first(k)
                route(X_A, m_a, on_a, sa_ref, xv[:, :HALF], sxa, rxa, d)
                route(X_B, m_b, on_b, sb_ref, xv[:, HALF:], sxb, rxb, d)

    low_lanes = lax.broadcasted_iota(jnp.int32, (SLOTS, 128), 1) < RANK

    def fold(rows, weights):
        product = lax.dot_general(rows, weights, (((1,), (1,)), ((), ())), preferred_element_type=F32)
        product = product * maskb[...].astype(F32)
        total = product[:, :128]
        for i in range(1, 8):
            total = total + product[:, i * 128 : (i + 1) * 128]
        return total + pltpu.roll(total, RANK, 1)

    def spread(both, is_a):
        wide = both.astype(F32)
        turned = pltpu.roll(wide, RANK, 1)
        one = (jnp.where(low_lanes, wide, turned) if is_a else jnp.where(low_lanes, turned, wide)).astype(BF)
        return jnp.concatenate([one] * 8, axis=1) * maskb[...]

    def over_z(relay_kind, final_kind, near_kind, far_kind, part, relay, final, everything, rows_a, weights_a, rows_b, weights_b):
        def one(i):
            t = zz(i)
            part[t] = jnp.where(
                low_lanes,
                fold(rows_a[t], weights_a[...].reshape(1024, -1)),
                fold(rows_b[t], weights_b[...].reshape(1024, -1)),
            )

        def begin():
            @pl.loop(3, 6)
            def _(i):
                one(i)

            copy(relay_kind, part.at[zz(-3)], relay.at[0], 0, 0, on_z(-1)).start()
            copy(relay_kind, part.at[zz(3)], relay.at[1], 1, 1, on_z(1)).start()
            copy(relay_kind, part.at[zz(4)], relay.at[2], 2, 2, on_z(2 * side)).start()

            @pl.loop(0, 2)
            def _(j):
                one(1 + 6 * j)

            copy(final_kind, part.at[zz(1)], final.at[0], 0, 0, on_z(1)).start()
            copy(final_kind, part.at[zz(-1)], final.at[1], 1, 1, on_z(-1)).start()

            @pl.loop(0, 3)
            def _(j):
                one(j * (j + 1))

        def pass_on():
            for i in range(3):
                arrived(relay_kind, relay.at[i], i)
            part[zz(-2)] += relay[0]
            part[zz(2)] += relay[1]
            part[zz(2 * side)] += relay[2]
            copy(final_kind, part.at[zz(2)], final.at[2], 2, 2, on_z(2)).start()
            copy(final_kind, part.at[zz(-2)], final.at[3], 3, 3, on_z(-2)).start()

        def publish():
            for i in range(4):
                arrived(final_kind, final.at[i], i)
            total = part[z] + final[0] + final[1] + final[2] + final[3]
            everything[z] = total.astype(BF)
            for i, step in enumerate((1, -1, 2, -2)):
                copy(near_kind, everything.at[z], everything.at[z], i, i, on_z(step)).start()

        def forward():
            arrived(near_kind, everything.at[zz(-2)], 2)
            arrived(near_kind, everything.at[zz(2)], 3)
            for i, (chunk, step) in enumerate(((-2, 1), (2, -1), (2 * side, -2 * side))):
                copy(far_kind, everything.at[zz(chunk)], everything.at[zz(chunk)], i, i, on_z(step)).start()

        def collect():
            arrived(near_kind, everything.at[zz(-1)], 0)
            arrived(near_kind, everything.at[zz(1)], 1)
            arrived(far_kind, everything.at[zz(-3)], 0)
            arrived(far_kind, everything.at[zz(3)], 1)
            arrived(far_kind, everything.at[zz(4)], 2)

        def finish():
            left(relay_kind, part.at[zz(-3)], 0)
            left(relay_kind, part.at[zz(3)], 1)
            left(relay_kind, part.at[zz(4)], 2)
            left(final_kind, part.at[zz(1)], 0)
            left(final_kind, part.at[zz(-1)], 1)
            left(final_kind, part.at[zz(2)], 2)
            left(final_kind, part.at[zz(-2)], 3)
            for i in range(4):
                left(near_kind, everything.at[z], i)
            for i in range(3):
                left(far_kind, everything.at[z], i)

        return begin, pass_on, publish, forward, collect, finish

    back = over_z(B_RELAY, B_FINAL, B_NEAR, B_FAR, bpart, brelay, bfinal, ball, rga, ua, rgb, ub)
    low = over_z(L_RELAY, L_FINAL, L_NEAR, L_FAR, lpart, lrelay, lfinal, lall, rxa, da, rxb, db)

    route_x(0, 4)

    with jax.named_scope("back_parts"):

        @pl.loop(1, 4)
        def _(d):
            fx = (x + d) % 4
            fy = (y + d) % 4
            arrived(U_A, ua.at[fx], fx)
            arrived(U_B, ub.at[fy], fy)

        @pl.loop(1, 8)
        def _(d):
            fa = (m_a + d) % 8
            fb = (m_b + d) % 8
            arrived(G_A, rga.at[fa], fa)
            arrived(G_B, rgb.at[fb], fb)

        back[0]()

    route_x(4, 8)
    with jax.named_scope("g_step_1"):
        g_step(1)
    with jax.named_scope("back_pass_on"):
        back[1]()
    with jax.named_scope("back_publish"):
        back[2]()
    with jax.named_scope("g_step_2"):
        g_step(2)
    with jax.named_scope("back_forward"):
        back[3]()
    with jax.named_scope("back_collect"):
        back[4]()

    with jax.named_scope("wait_d"):

        @pl.loop(1, 4)
        def _(d):
            fx = (x + d) % 4
            fy = (y + d) % 4
            arrived(D_A, da.at[fx], fx)
            arrived(D_B, db.at[fy], fy)

    def give_back(x_kind, kind, m, on, masked, is_a, weights, out, ret, d):
        s = (m + d) % 8
        block = spread(ball[s], is_a)
        masked[s] = block
        value = (
            adapter_scale * jnp.dot(block, weights[...].reshape(1024, HALF), preferred_element_type=F32)
        ).astype(BF)

        @pl.when(d != 0)
        def _():
            left(x_kind, out.at[s], s)
            out[s] = value
            copy(kind, out.at[s], ret.at[m], s, m, on(s)).start()

        @pl.when(d == 0)
        def _():
            ret[m] = value

    def give_back_all(lo, hi):
        with jax.named_scope("give_back"):

            @pl.loop(lo, hi)
            def _(k):
                d = near_first(k)
                give_back(X_A, R_A, m_a, on_a, ma, True, da, sxa, reta, d)
                give_back(X_B, R_B, m_b, on_b, mb, False, db, sxb, retb, d)

    give_back_all(0, 4)
    with jax.named_scope("g_step_3"):
        g_step(3)
    give_back_all(4, 8)

    with jax.named_scope("wait_x"):

        @pl.loop(1, 8)
        def _(d):
            fa = (m_a + d) % 8
            fb = (m_b + d) % 8
            arrived(X_A, rxa.at[fa], fa)
            arrived(X_B, rxb.at[fb], fb)

    with jax.named_scope("low_parts"):
        low[0]()

    def gradient(masked, rows, q):
        return adapter_scale * lax.dot_general(
            masked[:, :, pl.ds(pl.multiple_of(q * OWN, OWN), OWN)].reshape(8 * SLOTS, OWN),
            rows[...].reshape(8 * SLOTS, -1),
            (((0,), (0,)), ((), ())),
            preferred_element_type=F32,
        )

    def to_owner(kind, m, ring, masked, rows, part, recv, own, half, d):
        q = (m + d) % 4
        value = gradient(masked, rows, q)

        @pl.when(d == 4)
        def _():
            own[half] = value

        @pl.when(d != 4)
        def _():
            part[q] = value.astype(part.dtype)
            copy(kind, part.at[q], recv.at[m], q, m, ring(q)).start()

    with jax.named_scope("down_gradient"):

        @pl.loop(1, 5)
        def _(d):
            to_owner(DG_A, x, ring_x, ma, rxa, dga, dgra, dgo, 0, d)
            to_owner(DG_B, y, ring_y, mb, rxb, dgb, dgrb, dgo, 1, d)

    with jax.named_scope("low_pass_on"):
        low[1]()

    with jax.named_scope("frozen"):
        arrived(GR, g_half(-4, 0), 4)
        arrived(GL, g_half(4, 1), 4)
        w_in.wait()

        @pl.loop(0, ROWS // TILE)
        def _(i):
            rows = pl.ds(pl.multiple_of(i * TILE, TILE), TILE)
            acc[rows, :] = lax.dot_general(
                gfull[rows, :], wv[...], (((1,), (1,)), ((), ())), preferred_element_type=F32
            )

    with jax.named_scope("low_publish"):
        low[2]()

    lanes = lax.broadcasted_iota(jnp.int32, (TILE, SLOTS), 1)

    def take(pair_number, last):
        with jax.named_scope("take_back"):
            blocks = []
            for j in range(2):
                d = near_first(jnp.int32(2 * pair_number + j))
                ta = (m_a - d + 8) % 8
                tb = (m_b - d + 8) % 8

                @pl.when(d != 0)
                def _():
                    arrived(R_A, reta.at[ta], ta)
                    arrived(R_B, retb.at[tb], tb)

                blocks.append((ta, tb))

            @pl.loop(0, ROWS // TILE)
            def _(i):
                rows = pl.ds(pl.multiple_of(i * TILE, TILE), TILE)
                slots = cols[rows, :].astype(jnp.int32)
                for half, ret in enumerate((reta, retb)):
                    here = pl.ds(half * HALF, HALF)
                    total = acc[rows, here]
                    for ts in blocks:
                        t = ts[half]
                        pick = jnp.where(lanes + t * SLOTS == slots[:, half : half + 1], 1.0, 0.0).astype(BF)
                        total = total + jnp.dot(pick, ret[t], preferred_element_type=F32)
                    if last:
                        xv[rows, here] = total.astype(BF)
                    else:
                        acc[rows, here] = total
                if last:
                    pltpu.make_async_copy(xv.at[rows, :], out_hbm.at[rows, :], loc.at[2 + i]).start()

    take(0, False)
    with jax.named_scope("low_forward"):
        low[3]()
    take(1, False)

    with jax.named_scope("up_gradient"):
        low[4]()

        @pl.loop(0, 8)
        def _(s):
            ma[s] = spread(lall[s], True)
            mb[s] = spread(lall[s], False)

        @pl.loop(1, 5)
        def _(d):
            to_owner(UG_A, x, ring_x, ma, rga, uga, ugra, ugo, 0, d)
            to_owner(UG_B, y, ring_y, mb, rgb, ugb, ugrb, ugo, 1, d)

    take(2, False)
    take(3, True)

    with jax.named_scope("down_sum"):

        @pl.loop(1, 4)
        def _(d):
            fx = (x + d) % 4
            fy = (y + d) % 4
            arrived(DG_A, dgra.at[fx], fx)
            arrived(DG_B, dgrb.at[fy], fy)
            dgo[0] += dgra[fx].astype(F32)
            dgo[1] += dgrb[fy].astype(F32)

        down_ref[:, :HALF] = dgo[0]
        down_ref[:, HALF:] = dgo[1]

    with jax.named_scope("up_sum"):

        @pl.loop(1, 4)
        def _(d):
            fx = (x + d) % 4
            fy = (y + d) % 4
            arrived(UG_A, ugra.at[fx], fx)
            arrived(UG_B, ugrb.at[fy], fy)
            ugo[0] += ugra[fx]
            ugo[1] += ugrb[fy]

        up_ref[...] = ugo[0] + ugo[1]

    @pl.loop(1, 8)
    def _(d):
        ta = (m_a + d) % 8
        tb = (m_b + d) % 8
        left(G_A, sga.at[ta], ta)
        left(G_B, sgb.at[tb], tb)
        left(R_A, sxa.at[ta], ta)
        left(R_B, sxb.at[tb], tb)

    @pl.loop(1, 4)
    def _(d):
        tx = (x + d) % 4
        ty = (y + d) % 4
        left(U_A, u_ref, tx)
        left(U_B, u_ref, ty)
        left(D_A, d_ref.at[:, pl.ds(0, HALF)], tx)
        left(D_B, d_ref.at[:, pl.ds(HALF, HALF)], ty)
        left(DG_A, dga.at[tx], tx)
        left(DG_B, dgb.at[ty], ty)
        left(UG_A, uga.at[tx], tx)
        left(UG_B, ugb.at[ty], ty)

    back[5]()
    low[5]()
    left(GR, g_ref, 0)
    left(GL, g_ref, 0)
    for i in (1, 2):
        left(GR, g_whole(-i), i)
        left(GL, g_whole(i), i)
    left(GR, g_half(-3, 0), 3)
    left(GL, g_half(3, 1), 3)

    @pl.loop(0, ROWS // TILE)
    def _(i):
        rows = pl.ds(pl.multiple_of(i * TILE, TILE), TILE)
        pltpu.make_async_copy(xv.at[rows, :], out_hbm.at[rows, :], loc.at[2 + i]).wait()


def adapter_backward(ids, x, g, w, d, u):
    vmem = pl.BlockSpec(memory_space=pltpu.VMEM)
    hbm = pl.BlockSpec(memory_space=pl.ANY)

    def blocks(count, width, dtype=BF):
        return pltpu.VMEM((count, SLOTS, width), dtype)

    def chunk(width, dtype=BF):
        return pltpu.VMEM((4, OWN, width), dtype)

    sums = [blocks(8, 128, F32), blocks(3, 128, F32), blocks(4, 128, F32), blocks(8, 128)]
    return pl.pallas_call(
        adapter_kernel,
        out_shape=(
            jax.ShapeDtypeStruct((ROWS, 2 * HALF), BF),
            jax.ShapeDtypeStruct((OWN, 2 * HALF), F32),
            jax.ShapeDtypeStruct((OWN, GW), F32),
        ),
        in_specs=[vmem, hbm, vmem, hbm, vmem, vmem],
        out_specs=(hbm, vmem, vmem),
        scratch_shapes=[
            pltpu.VMEM((ROWS, 2 * HALF), BF), pltpu.VMEM((2 * HALF, 1024), BF),
            pltpu.VMEM((1, ROWS), jnp.int32), pltpu.VMEM((1, ROWS), jnp.int32), pltpu.VMEM((ROWS, 8), F32),
            blocks(8, HALF), blocks(8, HALF), blocks(8, GW), blocks(8, GW),
            blocks(8, HALF), blocks(8, HALF), blocks(8, GW), blocks(8, GW),
            chunk(HALF), chunk(HALF), chunk(GW), chunk(GW), pltpu.VMEM((SLOTS, 1024), BF),
            *sums, *sums,
            blocks(8, 1024), blocks(8, 1024), blocks(8, HALF), blocks(8, HALF),
            chunk(HALF), chunk(HALF), chunk(HALF), chunk(HALF), pltpu.VMEM((2, OWN, HALF), F32),
            chunk(GW, F32), chunk(GW, F32), chunk(GW, F32), chunk(GW, F32), pltpu.VMEM((2, OWN, GW), F32),
            pltpu.VMEM((ROWS, 1024), BF), pltpu.VMEM((ROWS, 2 * HALF), F32),
            pltpu.SemaphoreType.DMA((24, 8)), pltpu.SemaphoreType.DMA((24, 8)), pltpu.SemaphoreType.DMA((8,)),
        ],
        compiler_params=pltpu.CompilerParams(
            collective_id=0, has_side_effects=True, vmem_limit_bytes=62 * 2**20
        ),
        cost_estimate=pl.CostEstimate(flops=32 * 10**9, bytes_accessed=12 * 10**6, transcendentals=0),
        name="adapter_backward",
    )(ids, x, g, w, d, u)


def body(
    activations,
    output_gradient,
    adapter_of_row,
    frozen_value_weight,
    adapter_down_weight,
    adapter_up_weight,
):
    input_gradient, down, up = adapter_backward(
        adapter_of_row.reshape(1, ROWS),
        activations,
        output_gradient,
        frozen_value_weight,
        adapter_down_weight.reshape(OWN, 2 * HALF),
        adapter_up_weight.reshape(OWN, GW),
    )
    return input_gradient, down.reshape(4, RANK, 2 * HALF), up.reshape(4, RANK, GW)


def solution(mesh):
    in_specs = (
        P("adapter", "tensor"),
        P("adapter", "tensor"),
        P("adapter", None),
        P("tensor", None),
        P("adapter", None, "tensor"),
        P("adapter", None, "tensor"),
    )
    out_specs = (P("adapter", "tensor"), P("adapter", None, "tensor"), P("adapter", None, "tensor"))
    return jax.shard_map(body, mesh=mesh, in_specs=in_specs, out_specs=out_specs, check_vma=False)
```

```python
import jax
import jax.numpy as jnp
from jax import lax
from jax.experimental import pallas as pl
from jax.experimental.pallas import tpu as pltpu
from jax.sharding import PartitionSpec as P

adapter_scale = 2.0
MESH = pl.DeviceIdType.MESH
BF = jnp.bfloat16
F32 = jnp.float32

MOST = 15
SLOTS = 240
HALF = 512
ROWS = 1536
RANK = 64
GW = 128
OWN = 256
TILE = 256

(U_A, U_B, G_A, G_B, D_A, D_B, X_A, X_B, R_A, R_B, DG_A, DG_B, UG_A, UG_B, GR, GL,
 B_RELAY, B_FINAL, B_NEAR, B_FAR, L_RELAY, L_FINAL, L_NEAR, L_FAR, FU_A, FU_B, FD_A, FD_B) = range(28)


def adapter_kernel(
    ids_ref, x_hbm, g_ref, w_hbm, d_ref, u_ref,
    out_hbm, down_ref, up_ref,
    xv, wv, sa_ref, sb_ref, cols,
    sxa, sxb, sga, sgb, rxa, rxb, rga, rgb,
    da, db, ua, ub, maskb,
    bpart, brelay, bfinal, ball, lpart, lrelay, lfinal, lall,
    ma, mb, reta, retb,
    dga, dgb, dgra, dgrb, dgo, uga, ugb, ugra, ugrb, ugo,
    gfull, acc,
    ss, rs, loc,
):
    a = lax.axis_index("adapter")
    z = lax.axis_index("tensor")
    c = a % 2
    y = (a // 2) % 4
    x = a // 8
    m_a = y * 2 + c
    m_b = x * 2 + c
    side = 2 * (z % 2) - 1

    def on_a(t):
        return ((x * 4 + t // 2) * 2 + t % 2, z)

    def on_b(t):
        return (((t // 2) * 4 + y) * 2 + t % 2, z)

    def ring_x(t):
        return ((t * 4 + y) * 2 + c, z)

    def ring_y(t):
        return ((x * 4 + t) * 2 + c, z)

    def zz(i):
        return (z + i + 16) % 8

    def on_z(i):
        return (a, zz(i))

    def copy(kind, src, dst, to, me, device):
        return pltpu.make_async_remote_copy(
            src_ref=src, dst_ref=dst, send_sem=ss.at[kind, to], recv_sem=rs.at[kind, me],
            device_id=device, device_id_type=MESH,
        )

    def arrived(kind, dst, frm):
        copy(kind, dst, dst, frm, frm, (a, z)).wait_recv()

    def left(kind, src, to):
        copy(kind, src, src, to, to, (a, z)).wait_send()

    def near_first(k):
        return jnp.where(k < 4, 2 + 4 * (k % 2) + k // 2, 4 * (1 - (k - 4) // 2) + k % 2)

    x_in = pltpu.make_async_copy(x_hbm, xv, loc.at[0])
    x_in.start()
    w_in = pltpu.make_async_copy(w_hbm, wv, loc.at[1])
    w_in.start()

    barrier = pltpu.get_barrier_semaphore()

    @pl.loop(1, 8)
    def _(d):
        pl.semaphore_signal(barrier, inc=1, device_id=on_a((m_a + d) % 8), device_id_type=MESH)
        pl.semaphore_signal(barrier, inc=1, device_id=on_z(d), device_id_type=MESH)

    @pl.loop(2, 8)
    def _(d):
        t = ((x * 2) + d) % 8
        pl.semaphore_signal(barrier, inc=1, device_id=on_b(t), device_id_type=MESH)

    with jax.named_scope("slots"):
        ids = ids_ref[...]
        hot = jnp.where(lax.broadcasted_iota(jnp.int32, (128, ROWS), 0) == ids, 1.0, 0.0)
        before = jnp.where(
            lax.broadcasted_iota(jnp.int32, (TILE, TILE), 0) < lax.broadcasted_iota(jnp.int32, (TILE, TILE), 1), 1.0, 0.0
        ).astype(BF)
        seen = jnp.zeros((128, 1), F32)
        places = []
        for q in range(ROWS // TILE):
            part = hot[:, q * TILE : (q + 1) * TILE]
            count = jnp.dot(part.astype(BF), before, preferred_element_type=F32) + seen
            places.append(jnp.sum(count * part, axis=0, keepdims=True))
            seen = seen + jnp.sum(part, axis=1, keepdims=True)
        place = jnp.concatenate(places, axis=1).astype(jnp.int32)
        owner, within = ids >> 2, ids & 3
        core, oy, ox = owner & 1, (owner >> 1) & 3, owner >> 3
        slot_a = (oy * 2 + core) * SLOTS + (ox * 4 + within) * MOST + place
        slot_b = (ox * 2 + core) * SLOTS + (oy * 4 + within) * MOST + place
        sa_ref[...] = slot_a
        sb_ref[...] = slot_b
        cols[...] = jnp.concatenate([slot_a.astype(F32), slot_b.astype(F32)] * 4, axis=0).T

        first = (lax.broadcasted_iota(jnp.int32, (SLOTS, 1024), 1) >> 6) * MOST
        row = lax.broadcasted_iota(jnp.int32, (SLOTS, 1024), 0)
        maskb[...] = jnp.where((row >= first) & (row < first + MOST), 1.0, 0.0).astype(BF)

    pl.semaphore_wait(barrier, 20)

    def spread_ring(kind_a, kind_b, src_a, src_b, dst_a, dst_b):
        for d in (1, 3):
            tx = (x + d) % 4
            ty = (y + d) % 4
            copy(kind_a, src_a, dst_a.at[x], tx, x, ring_x(tx)).start()
            copy(kind_b, src_b, dst_b.at[y], ty, y, ring_y(ty)).start()

    def upper(ref, t):
        return ref.at[t, pl.ds(0, OWN // 2), :]

    def lower(ref, t):
        return ref.at[t, pl.ds(OWN // 2, OWN // 2), :]

    def forward_ring(kind, far_kind, dst, m, ring):
        before, after = (m + 3) % 4, (m + 1) % 4
        arrived(kind, dst.at[before], before)
        arrived(kind, dst.at[after], after)
        copy(far_kind, upper(dst, before), upper(dst, before), 0, 0, ring(after)).start()
        copy(far_kind, lower(dst, after), lower(dst, after), 1, 1, ring(before)).start()

    def opposite_ring(far_kind, dst, m):
        across = (m + 2) % 4
        arrived(far_kind, upper(dst, across), 0)
        arrived(far_kind, lower(dst, across), 1)

    spread_ring(U_A, U_B, u_ref, u_ref, ua, ub)
    ua[x] = u_ref[...]
    ub[y] = u_ref[...]

    def g_cols(i):
        return pl.ds(pl.multiple_of(zz(i) * GW, GW), GW)

    def g_whole(i):
        return gfull.at[:, g_cols(i)]

    def g_half(i, upper):
        return gfull.at[pl.ds(upper * (ROWS // 2), ROWS // 2), g_cols(i)]

    copy(GR, g_ref, g_whole(0), 0, 1, on_z(1)).start()
    copy(GL, g_ref, g_whole(0), 0, 1, on_z(-1)).start()

    def g_step(i):
        arrived(GR, g_whole(-i), i)
        arrived(GL, g_whole(i), i)
        if i < 3:
            copy(GR, g_whole(-i), g_whole(-i), i, i + 1, on_z(1)).start()
            copy(GL, g_whole(i), g_whole(i), i, i + 1, on_z(-1)).start()
        else:
            copy(GR, g_half(-i, 0), g_half(-i, 0), i, i + 1, on_z(1)).start()
            copy(GL, g_half(i, 1), g_half(i, 1), i, i + 1, on_z(-1)).start()

    slot_rows = lax.broadcasted_iota(jnp.int32, (SLOTS, ROWS), 0)

    def choose(s_ref, t):
        return jnp.where(slot_rows + t * SLOTS == s_ref[...], 1.0, 0.0).astype(BF)

    def route(kind, m, on, s_ref, value, send, recv, d, hold=False):
        t = (m + d) % 8
        block = jnp.dot(choose(s_ref, t), value, preferred_element_type=F32).astype(BF)

        @pl.when(d == 0)
        def _():
            recv[m] = block

        @pl.when(d != 0)
        def _():
            send[t] = block
            if not hold:
                copy(kind, send.at[t], recv.at[m], t, m, on(t)).start()

    with jax.named_scope("route_g"):

        @pl.loop(0, 8)
        def _(k):
            d = near_first(k)
            route(G_A, m_a, on_a, sa_ref, g_ref[...], sga, rga, d)
            route(G_B, m_b, on_b, sb_ref, g_ref[...], sgb, rgb, d)

    gfull[:, g_cols(0)] = g_ref[...]

    spread_ring(D_A, D_B, d_ref.at[:, pl.ds(0, HALF)], d_ref.at[:, pl.ds(HALF, HALF)], da, db)
    forward_ring(U_A, FU_A, ua, x, ring_x)
    forward_ring(U_B, FU_B, ub, y, ring_y)
    da[x] = d_ref[:, :HALF]
    db[y] = d_ref[:, HALF:]
    x_in.wait()

    def route_x(lo, hi, hold=False):
        with jax.named_scope("route_x"):

            @pl.loop(lo, hi)
            def _(k):
                d = near_first(k)
                route(X_A, m_a, on_a, sa_ref, xv[:, :HALF], sxa, rxa, d, hold)
                route(X_B, m_b, on_b, sb_ref, xv[:, HALF:], sxb, rxb, d, hold)

    def release_x(lo, hi):
        @pl.loop(lo, hi)
        def _(k):
            d = near_first(k)
            ta = (m_a + d) % 8
            tb = (m_b + d) % 8
            copy(X_A, sxa.at[ta], rxa.at[m_a], ta, m_a, on_a(ta)).start()
            copy(X_B, sxb.at[tb], rxb.at[m_b], tb, m_b, on_b(tb)).start()

    low_lanes = lax.broadcasted_iota(jnp.int32, (SLOTS, 128), 1) < RANK

    def fold(rows, weights):
        product = lax.dot_general(rows, weights, (((1,), (1,)), ((), ())), preferred_element_type=F32)
        product = product * maskb[...].astype(F32)
        total = product[:, :128]
        for i in range(1, 8):
            total = total + product[:, i * 128 : (i + 1) * 128]
        return total + pltpu.roll(total, RANK, 1)

    def spread(both, is_a):
        wide = both.astype(F32)
        turned = pltpu.roll(wide, RANK, 1)
        one = (jnp.where(low_lanes, wide, turned) if is_a else jnp.where(low_lanes, turned, wide)).astype(BF)
        return jnp.concatenate([one] * 8, axis=1) * maskb[...]

    def over_z(relay_kind, final_kind, near_kind, far_kind, part, relay, final, everything, rows_a, weights_a, rows_b, weights_b):
        def one(i):
            t = zz(i)
            part[t] = jnp.where(
                low_lanes,
                fold(rows_a[t], weights_a[...].reshape(1024, -1)),
                fold(rows_b[t], weights_b[...].reshape(1024, -1)),
            )

        def begin():
            @pl.loop(3, 6)
            def _(i):
                one(i)

            copy(relay_kind, part.at[zz(-3)], relay.at[0], 0, 0, on_z(-1)).start()
            copy(relay_kind, part.at[zz(3)], relay.at[1], 1, 1, on_z(1)).start()
            copy(relay_kind, part.at[zz(4)], relay.at[2], 2, 2, on_z(2 * side)).start()

            @pl.loop(0, 2)
            def _(j):
                one(1 + 6 * j)

            copy(final_kind, part.at[zz(1)], final.at[0], 0, 0, on_z(1)).start()
            copy(final_kind, part.at[zz(-1)], final.at[1], 1, 1, on_z(-1)).start()

            @pl.loop(0, 3)
            def _(j):
                one(j * (j + 1))

        def pass_on():
            for i in range(3):
                arrived(relay_kind, relay.at[i], i)
            part[zz(-2)] += relay[0]
            part[zz(2)] += relay[1]
            part[zz(2 * side)] += relay[2]
            copy(final_kind, part.at[zz(2)], final.at[2], 2, 2, on_z(2)).start()
            copy(final_kind, part.at[zz(-2)], final.at[3], 3, 3, on_z(-2)).start()

        def publish():
            for i in range(4):
                arrived(final_kind, final.at[i], i)
            total = part[z] + final[0] + final[1] + final[2] + final[3]
            everything[z] = total.astype(BF)
            for i, step in enumerate((1, -1, 2, -2)):
                copy(near_kind, everything.at[z], everything.at[z], i, i, on_z(step)).start()

        def forward():
            arrived(near_kind, everything.at[zz(-2)], 2)
            arrived(near_kind, everything.at[zz(2)], 3)
            for i, (chunk, step) in enumerate(((-2, 1), (2, -1), (2 * side, -2 * side))):
                copy(far_kind, everything.at[zz(chunk)], everything.at[zz(chunk)], i, i, on_z(step)).start()

        def collect():
            arrived(near_kind, everything.at[zz(-1)], 0)
            arrived(near_kind, everything.at[zz(1)], 1)
            arrived(far_kind, everything.at[zz(-3)], 0)
            arrived(far_kind, everything.at[zz(3)], 1)
            arrived(far_kind, everything.at[zz(4)], 2)

        def finish():
            left(relay_kind, part.at[zz(-3)], 0)
            left(relay_kind, part.at[zz(3)], 1)
            left(relay_kind, part.at[zz(4)], 2)
            left(final_kind, part.at[zz(1)], 0)
            left(final_kind, part.at[zz(-1)], 1)
            left(final_kind, part.at[zz(2)], 2)
            left(final_kind, part.at[zz(-2)], 3)
            for i in range(4):
                left(near_kind, everything.at[z], i)
            for i in range(3):
                left(far_kind, everything.at[z], i)

        return begin, pass_on, publish, forward, collect, finish

    back = over_z(B_RELAY, B_FINAL, B_NEAR, B_FAR, bpart, brelay, bfinal, ball, rga, ua, rgb, ub)
    low = over_z(L_RELAY, L_FINAL, L_NEAR, L_FAR, lpart, lrelay, lfinal, lall, rxa, da, rxb, db)

    route_x(0, 2, hold=True)
    opposite_ring(FU_A, ua, x)
    opposite_ring(FU_B, ub, y)

    @pl.loop(1, 8)
    def _(d):
        fa = (m_a + d) % 8
        fb = (m_b + d) % 8
        arrived(G_A, rga.at[fa], fa)
        arrived(G_B, rgb.at[fb], fb)

    release_x(0, 2)
    back[0]()
    route_x(2, 4)
    back[1]()
    route_x(4, 6)
    back[2]()
    route_x(6, 8)
    back[3]()
    forward_ring(D_A, FD_A, da, x, ring_x)
    forward_ring(D_B, FD_B, db, y, ring_y)
    back[4]()
    g_step(1)
    opposite_ring(FD_A, da, x)
    opposite_ring(FD_B, db, y)

    def give_back(x_kind, kind, m, on, masked, is_a, weights, out, ret, d):
        s = (m + d) % 8
        block = spread(ball[s], is_a)
        masked[s] = block
        value = (
            adapter_scale * jnp.dot(block, weights[...].reshape(1024, HALF), preferred_element_type=F32)
        ).astype(BF)

        @pl.when(d != 0)
        def _():
            left(x_kind, out.at[s], s)
            out[s] = value
            copy(kind, out.at[s], ret.at[m], s, m, on(s)).start()

        @pl.when(d == 0)
        def _():
            ret[m] = value

    def give_back_all(lo, hi):
        with jax.named_scope("give_back"):

            @pl.loop(lo, hi)
            def _(k):
                d = near_first(k)
                give_back(X_A, R_A, m_a, on_a, ma, True, da, sxa, reta, d)
                give_back(X_B, R_B, m_b, on_b, mb, False, db, sxb, retb, d)

    give_back_all(0, 8)
    g_step(2)

    with jax.named_scope("wait_x"):

        @pl.loop(1, 8)
        def _(d):
            fa = (m_a + d) % 8
            fb = (m_b + d) % 8
            arrived(X_A, rxa.at[fa], fa)
            arrived(X_B, rxb.at[fb], fb)

    with jax.named_scope("low_parts"):
        low[0]()

    def gradient(masked, rows, q):
        return adapter_scale * lax.dot_general(
            masked[:, :, pl.ds(pl.multiple_of(q * OWN, OWN), OWN)].reshape(8 * SLOTS, OWN),
            rows[...].reshape(8 * SLOTS, -1),
            (((0,), (0,)), ((), ())),
            preferred_element_type=F32,
        )

    def to_owners(kind, m, ring, masked, rows, part, recv, own, half, first):
        across, after, before = (m + 2) % 4, (m + 1) % 4, (m + 3) % 4
        if first:
            part[across] = gradient(masked, rows, across).astype(part.dtype)
            copy(kind, upper(part, across), upper(recv, 2), 2, 2, ring(after)).start()
            copy(kind, lower(part, across), lower(recv, 2), 3, 3, ring(before)).start()
            own[half] = gradient(masked, rows, m)
        else:
            for t, slot, edge, at in ((after, 0, upper, 0), (before, 1, lower, OWN // 2)):
                value = gradient(masked, rows, t)
                arrived(kind, edge(recv, 2), 2 + slot)
                part[t] = value.astype(part.dtype)
                rows_of = pl.ds(at, OWN // 2)
                part[t, rows_of, :] = (
                    value[at : at + OWN // 2] + recv[2, rows_of, :].astype(F32)
                ).astype(part.dtype)
                copy(kind, part.at[t], recv.at[slot], slot, slot, ring(t)).start()

    def from_neighbours(kind, recv, own, half):
        for slot in range(2):
            arrived(kind, recv.at[slot], slot)
        own[half] += recv[0].astype(F32) + recv[1].astype(F32)

    def sent_to_owners(kind, m, part):
        across = (m + 2) % 4
        left(kind, part.at[0], 0)
        left(kind, part.at[0], 1)
        left(kind, upper(part, across), 2)
        left(kind, lower(part, across), 3)

    def down_gradient(first):
        with jax.named_scope("down_gradient"):
            to_owners(DG_A, x, ring_x, ma, rxa, dga, dgra, dgo, 0, first)
            to_owners(DG_B, y, ring_y, mb, rxb, dgb, dgrb, dgo, 1, first)

    low[1]()
    down_gradient(True)
    g_step(3)
    low[2]()

    with jax.named_scope("frozen"):
        arrived(GR, g_half(-4, 0), 4)
        arrived(GL, g_half(4, 1), 4)
        w_in.wait()

        @pl.loop(0, ROWS // TILE)
        def _(i):
            rows = pl.ds(pl.multiple_of(i * TILE, TILE), TILE)
            acc[rows, :] = lax.dot_general(
                gfull[rows, :], wv[...], (((1,), (1,)), ((), ())), preferred_element_type=F32
            )

    low[3]()

    lanes = lax.broadcasted_iota(jnp.int32, (TILE, SLOTS), 1)

    def take(pair_number, last):
        with jax.named_scope("take_back"):
            blocks = []
            for j in range(2):
                d = near_first(jnp.int32(2 * pair_number + j))
                ta = (m_a - d + 8) % 8
                tb = (m_b - d + 8) % 8

                @pl.when(d != 0)
                def _():
                    arrived(R_A, reta.at[ta], ta)
                    arrived(R_B, retb.at[tb], tb)

                blocks.append((ta, tb))

            @pl.loop(0, ROWS // TILE)
            def _(i):
                rows = pl.ds(pl.multiple_of(i * TILE, TILE), TILE)
                slots = cols[rows, :].astype(jnp.int32)
                for half, ret in enumerate((reta, retb)):
                    here = pl.ds(half * HALF, HALF)
                    total = acc[rows, here]
                    for ts in blocks:
                        t = ts[half]
                        pick = jnp.where(lanes + t * SLOTS == slots[:, half : half + 1], 1.0, 0.0).astype(BF)
                        total = total + jnp.dot(pick, ret[t], preferred_element_type=F32)
                    if last:
                        xv[rows, here] = total.astype(BF)
                    else:
                        acc[rows, here] = total
                if last:
                    pltpu.make_async_copy(xv.at[rows, :], out_hbm.at[rows, :], loc.at[2 + i]).start()

    def to_owner(kind, m, ring, masked, rows, part, recv, own, half, d):
        q = (m + d) % 4
        value = gradient(masked, rows, q)

        @pl.when(d == 4)
        def _():
            own[half] = value

        @pl.when(d != 4)
        def _():
            part[q] = value
            copy(kind, part.at[q], recv.at[m], q, m, ring(q)).start()

    take(0, False)
    take(1, False)
    down_gradient(False)
    take(2, False)
    take(3, True)
    low[4]()

    with jax.named_scope("up_gradient"):

        @pl.loop(0, 8)
        def _(s):
            ma[s] = spread(lall[s], True)
            mb[s] = spread(lall[s], False)

        @pl.loop(1, 5)
        def _(d):
            to_owner(UG_A, x, ring_x, ma, rga, uga, ugra, ugo, 0, d)
            to_owner(UG_B, y, ring_y, mb, rgb, ugb, ugrb, ugo, 1, d)

    with jax.named_scope("down_sum"):
        from_neighbours(DG_A, dgra, dgo, 0)
        from_neighbours(DG_B, dgrb, dgo, 1)
        down_ref[:, :HALF] = dgo[0]
        down_ref[:, HALF:] = dgo[1]

    with jax.named_scope("up_sum"):

        @pl.loop(1, 4)
        def _(d):
            fx = (x + d) % 4
            fy = (y + d) % 4
            arrived(UG_A, ugra.at[fx], fx)
            arrived(UG_B, ugrb.at[fy], fy)
            ugo[0] += ugra[fx]
            ugo[1] += ugrb[fy]

        up_ref[...] = ugo[0] + ugo[1]

    @pl.loop(1, 8)
    def _(d):
        ta = (m_a + d) % 8
        tb = (m_b + d) % 8
        left(G_A, sga.at[ta], ta)
        left(G_B, sgb.at[tb], tb)
        left(R_A, sxa.at[ta], ta)
        left(R_B, sxb.at[tb], tb)

    for d in (1, 3):
        tx = (x + d) % 4
        ty = (y + d) % 4
        left(U_A, u_ref, tx)
        left(U_B, u_ref, ty)
        left(D_A, d_ref.at[:, pl.ds(0, HALF)], tx)
        left(D_B, d_ref.at[:, pl.ds(HALF, HALF)], ty)
    for i in range(2):
        left(FU_A, upper(ua, 0), i)
        left(FU_B, upper(ub, 0), i)
        left(FD_A, upper(da, 0), i)
        left(FD_B, upper(db, 0), i)
    sent_to_owners(DG_A, x, dga)
    sent_to_owners(DG_B, y, dgb)

    @pl.loop(1, 4)
    def _(d):
        left(UG_A, uga.at[(x + d) % 4], (x + d) % 4)
        left(UG_B, ugb.at[(y + d) % 4], (y + d) % 4)


    back[5]()
    low[5]()
    left(GR, g_ref, 0)
    left(GL, g_ref, 0)
    for i in (1, 2):
        left(GR, g_whole(-i), i)
        left(GL, g_whole(i), i)
    left(GR, g_half(-3, 0), 3)
    left(GL, g_half(3, 1), 3)

    @pl.loop(0, ROWS // TILE)
    def _(i):
        rows = pl.ds(pl.multiple_of(i * TILE, TILE), TILE)
        pltpu.make_async_copy(xv.at[rows, :], out_hbm.at[rows, :], loc.at[2 + i]).wait()


def adapter_backward(ids, x, g, w, d, u):
    vmem = pl.BlockSpec(memory_space=pltpu.VMEM)
    hbm = pl.BlockSpec(memory_space=pl.ANY)

    def blocks(count, width, dtype=BF):
        return pltpu.VMEM((count, SLOTS, width), dtype)

    def chunk(width, dtype=BF):
        return pltpu.VMEM((4, OWN, width), dtype)

    sums = [blocks(8, 128, F32), blocks(3, 128, F32), blocks(4, 128, F32), blocks(8, 128)]
    return pl.pallas_call(
        adapter_kernel,
        out_shape=(
            jax.ShapeDtypeStruct((ROWS, 2 * HALF), BF),
            jax.ShapeDtypeStruct((OWN, 2 * HALF), F32),
            jax.ShapeDtypeStruct((OWN, GW), F32),
        ),
        in_specs=[vmem, hbm, vmem, hbm, vmem, vmem],
        out_specs=(hbm, vmem, vmem),
        scratch_shapes=[
            pltpu.VMEM((ROWS, 2 * HALF), BF), pltpu.VMEM((2 * HALF, 1024), BF),
            pltpu.VMEM((1, ROWS), jnp.int32), pltpu.VMEM((1, ROWS), jnp.int32), pltpu.VMEM((ROWS, 8), F32),
            blocks(8, HALF), blocks(8, HALF), blocks(8, GW), blocks(8, GW),
            blocks(8, HALF), blocks(8, HALF), blocks(8, GW), blocks(8, GW),
            chunk(HALF), chunk(HALF), chunk(GW), chunk(GW), pltpu.VMEM((SLOTS, 1024), BF),
            *sums, *sums,
            blocks(8, 1024), blocks(8, 1024), blocks(8, HALF), blocks(8, HALF),
            chunk(HALF), chunk(HALF), chunk(HALF), chunk(HALF), pltpu.VMEM((2, OWN, HALF), F32),
            chunk(GW, F32), chunk(GW, F32), chunk(GW, F32), chunk(GW, F32), pltpu.VMEM((2, OWN, GW), F32),
            pltpu.VMEM((ROWS, 1024), BF), pltpu.VMEM((ROWS, 2 * HALF), F32),
            pltpu.SemaphoreType.DMA((28, 8)), pltpu.SemaphoreType.DMA((28, 8)), pltpu.SemaphoreType.DMA((8,)),
        ],
        compiler_params=pltpu.CompilerParams(
            collective_id=0, has_side_effects=True, vmem_limit_bytes=62 * 2**20
        ),
        cost_estimate=pl.CostEstimate(flops=32 * 10**9, bytes_accessed=12 * 10**6, transcendentals=0),
        name="adapter_backward",
    )(ids, x, g, w, d, u)


def body(
    activations,
    output_gradient,
    adapter_of_row,
    frozen_value_weight,
    adapter_down_weight,
    adapter_up_weight,
):
    input_gradient, down, up = adapter_backward(
        adapter_of_row.reshape(1, ROWS),
        activations,
        output_gradient,
        frozen_value_weight,
        adapter_down_weight.reshape(OWN, 2 * HALF),
        adapter_up_weight.reshape(OWN, GW),
    )
    return input_gradient, down.reshape(4, RANK, 2 * HALF), up.reshape(4, RANK, GW)


def solution(mesh):
    in_specs = (
        P("adapter", "tensor"),
        P("adapter", "tensor"),
        P("adapter", None),
        P("tensor", None),
        P("adapter", None, "tensor"),
        P("adapter", None, "tensor"),
    )
    out_specs = (P("adapter", "tensor"), P("adapter", None, "tensor"), P("adapter", None, "tensor"))
    return jax.shard_map(body, mesh=mesh, in_specs=in_specs, out_specs=out_specs, check_vma=False)
```

```python
import jax
import jax.numpy as jnp
from jax import lax
from jax.experimental import pallas as pl
from jax.experimental.pallas import tpu as pltpu
from jax.sharding import PartitionSpec as P

adapter_scale = 2.0
MESH = pl.DeviceIdType.MESH
BF = jnp.bfloat16
F32 = jnp.float32

MOST = 15
SLOTS = 240
HALF = 512
ROWS = 1536
RANK = 64
GW = 128
OWN = 256
TILE = 256

(U_A, U_B, G_A, G_B, D_A, D_B, X_A, X_B, R_A, R_B, DG_A, DG_B, UG_A, UG_B, GR, GL,
 B_RELAY, B_FINAL, B_NEAR, B_FAR, L_RELAY, L_FINAL, L_NEAR, L_FAR, FU_A, FU_B, FD_A, FD_B) = range(28)


def adapter_kernel(
    ids_ref, x_hbm, g_ref, w_hbm, d_ref, u_ref,
    out_hbm, down_ref, up_ref,
    xv, wv, sa_ref, sb_ref, cols,
    sxa, sxb, sga, sgb, rxa, rxb, rga, rgb,
    da, db, ua, ub, maskb,
    bpart, brelay, bfinal, ball, lpart, lrelay, lfinal, lall,
    ma, mb, reta, retb,
    dga, dgb, dgra, dgrb, dgo, uga, ugb, ugra, ugrb, ugo,
    gfull, acc,
    ss, rs, loc,
):
    a = lax.axis_index("adapter")
    z = lax.axis_index("tensor")
    c = a % 2
    y = (a // 2) % 4
    x = a // 8
    m_a = y * 2 + c
    m_b = x * 2 + c
    side = 2 * (z % 2) - 1

    def on_a(t):
        return ((x * 4 + t // 2) * 2 + t % 2, z)

    def on_b(t):
        return (((t // 2) * 4 + y) * 2 + t % 2, z)

    def ring_x(t):
        return ((t * 4 + y) * 2 + c, z)

    def ring_y(t):
        return ((x * 4 + t) * 2 + c, z)

    def zz(i):
        return (z + i + 16) % 8

    def on_z(i):
        return (a, zz(i))

    def copy(kind, src, dst, to, me, device):
        return pltpu.make_async_remote_copy(
            src_ref=src, dst_ref=dst, send_sem=ss.at[kind, to], recv_sem=rs.at[kind, me],
            device_id=device, device_id_type=MESH,
        )

    def arrived(kind, dst, frm):
        copy(kind, dst, dst, frm, frm, (a, z)).wait_recv()

    def left(kind, src, to):
        copy(kind, src, src, to, to, (a, z)).wait_send()

    def near_first(k):
        return jnp.where(k < 4, 2 + 4 * (k % 2) + k // 2, 4 * (1 - (k - 4) // 2) + k % 2)

    x_in = pltpu.make_async_copy(x_hbm, xv, loc.at[0])
    x_in.start()
    w_in = pltpu.make_async_copy(w_hbm, wv, loc.at[1])
    w_in.start()

    barrier = pltpu.get_barrier_semaphore()

    @pl.loop(1, 8)
    def _(d):
        pl.semaphore_signal(barrier, inc=1, device_id=on_a((m_a + d) % 8), device_id_type=MESH)
        pl.semaphore_signal(barrier, inc=1, device_id=on_z(d), device_id_type=MESH)

    @pl.loop(2, 8)
    def _(d):
        t = ((x * 2) + d) % 8
        pl.semaphore_signal(barrier, inc=1, device_id=on_b(t), device_id_type=MESH)

    with jax.named_scope("slots"):
        ids = ids_ref[...]
        hot = jnp.where(lax.broadcasted_iota(jnp.int32, (128, ROWS), 0) == ids, 1.0, 0.0)
        before = jnp.where(
            lax.broadcasted_iota(jnp.int32, (TILE, TILE), 0) < lax.broadcasted_iota(jnp.int32, (TILE, TILE), 1), 1.0, 0.0
        ).astype(BF)
        seen = jnp.zeros((128, 1), F32)
        places = []
        for q in range(ROWS // TILE):
            part = hot[:, q * TILE : (q + 1) * TILE]
            count = jnp.dot(part.astype(BF), before, preferred_element_type=F32) + seen
            places.append(jnp.sum(count * part, axis=0, keepdims=True))
            seen = seen + jnp.sum(part, axis=1, keepdims=True)
        place = jnp.concatenate(places, axis=1).astype(jnp.int32)
        owner, within = ids >> 2, ids & 3
        core, oy, ox = owner & 1, (owner >> 1) & 3, owner >> 3
        slot_a = (oy * 2 + core) * SLOTS + (ox * 4 + within) * MOST + place
        slot_b = (ox * 2 + core) * SLOTS + (oy * 4 + within) * MOST + place
        sa_ref[...] = slot_a
        sb_ref[...] = slot_b
        cols[...] = jnp.concatenate([slot_a.astype(F32), slot_b.astype(F32)] * 4, axis=0).T

        first = (lax.broadcasted_iota(jnp.int32, (SLOTS, 1024), 1) >> 6) * MOST
        row = lax.broadcasted_iota(jnp.int32, (SLOTS, 1024), 0)
        maskb[...] = jnp.where((row >= first) & (row < first + MOST), 1.0, 0.0).astype(BF)

    pl.semaphore_wait(barrier, 20)

    def spread_ring(kind_a, kind_b, src_a, src_b, dst_a, dst_b):
        for d in (1, 3):
            tx = (x + d) % 4
            ty = (y + d) % 4
            copy(kind_a, src_a, dst_a.at[x], tx, x, ring_x(tx)).start()
            copy(kind_b, src_b, dst_b.at[y], ty, y, ring_y(ty)).start()

    def upper(ref, t):
        return ref.at[t, pl.ds(0, OWN // 2), :]

    def lower(ref, t):
        return ref.at[t, pl.ds(OWN // 2, OWN // 2), :]

    def forward_ring(kind, far_kind, dst, m, ring):
        before, after = (m + 3) % 4, (m + 1) % 4
        arrived(kind, dst.at[before], before)
        arrived(kind, dst.at[after], after)
        copy(far_kind, upper(dst, before), upper(dst, before), 0, 0, ring(after)).start()
        copy(far_kind, lower(dst, after), lower(dst, after), 1, 1, ring(before)).start()

    def opposite_ring(far_kind, dst, m):
        across = (m + 2) % 4
        arrived(far_kind, upper(dst, across), 0)
        arrived(far_kind, lower(dst, across), 1)

    spread_ring(U_A, U_B, u_ref, u_ref, ua, ub)
    ua[x] = u_ref[...]
    ub[y] = u_ref[...]

    def g_cols(i):
        return pl.ds(pl.multiple_of(zz(i) * GW, GW), GW)

    def g_whole(i):
        return gfull.at[:, g_cols(i)]

    def g_half(i, upper):
        return gfull.at[pl.ds(upper * (ROWS // 2), ROWS // 2), g_cols(i)]

    copy(GR, g_ref, g_whole(0), 0, 1, on_z(1)).start()
    copy(GL, g_ref, g_whole(0), 0, 1, on_z(-1)).start()

    def g_step(i):
        arrived(GR, g_whole(-i), i)
        arrived(GL, g_whole(i), i)
        if i < 3:
            copy(GR, g_whole(-i), g_whole(-i), i, i + 1, on_z(1)).start()
            copy(GL, g_whole(i), g_whole(i), i, i + 1, on_z(-1)).start()
        else:
            copy(GR, g_half(-i, 0), g_half(-i, 0), i, i + 1, on_z(1)).start()
            copy(GL, g_half(i, 1), g_half(i, 1), i, i + 1, on_z(-1)).start()

    slot_rows = lax.broadcasted_iota(jnp.int32, (SLOTS, ROWS), 0)

    def choose(s_ref, t):
        return jnp.where(slot_rows + t * SLOTS == s_ref[...], 1.0, 0.0).astype(BF)

    def route(kind, m, on, s_ref, value, send, recv, d, hold=False):
        t = (m + d) % 8
        block = jnp.dot(choose(s_ref, t), value, preferred_element_type=F32).astype(BF)

        @pl.when(d == 0)
        def _():
            recv[m] = block

        @pl.when(d != 0)
        def _():
            send[t] = block
            if not hold:
                copy(kind, send.at[t], recv.at[m], t, m, on(t)).start()

    with jax.named_scope("route_g"):

        @pl.loop(0, 8)
        def _(k):
            d = near_first(k)
            route(G_A, m_a, on_a, sa_ref, g_ref[...], sga, rga, d)
            route(G_B, m_b, on_b, sb_ref, g_ref[...], sgb, rgb, d)

    gfull[:, g_cols(0)] = g_ref[...]

    forward_ring(U_A, FU_A, ua, x, ring_x)
    forward_ring(U_B, FU_B, ub, y, ring_y)
    da[x] = d_ref[:, :HALF]
    db[y] = d_ref[:, HALF:]
    x_in.wait()

    def route_x(lo, hi, hold=False):
        with jax.named_scope("route_x"):

            @pl.loop(lo, hi)
            def _(k):
                d = near_first(k)
                route(X_A, m_a, on_a, sa_ref, xv[:, :HALF], sxa, rxa, d, hold)
                route(X_B, m_b, on_b, sb_ref, xv[:, HALF:], sxb, rxb, d, hold)

    def release_x(lo, hi):
        @pl.loop(lo, hi)
        def _(k):
            d = near_first(k)
            ta = (m_a + d) % 8
            tb = (m_b + d) % 8
            copy(X_A, sxa.at[ta], rxa.at[m_a], ta, m_a, on_a(ta)).start()
            copy(X_B, sxb.at[tb], rxb.at[m_b], tb, m_b, on_b(tb)).start()

    low_lanes = lax.broadcasted_iota(jnp.int32, (SLOTS, 128), 1) < RANK

    def fold(rows, weights):
        product = lax.dot_general(rows, weights, (((1,), (1,)), ((), ())), preferred_element_type=F32)
        product = product * maskb[...].astype(F32)
        total = product[:, :128]
        for i in range(1, 8):
            total = total + product[:, i * 128 : (i + 1) * 128]
        return total + pltpu.roll(total, RANK, 1)

    def spread(both, is_a):
        wide = both.astype(F32)
        turned = pltpu.roll(wide, RANK, 1)
        one = (jnp.where(low_lanes, wide, turned) if is_a else jnp.where(low_lanes, turned, wide)).astype(BF)
        return jnp.concatenate([one] * 8, axis=1) * maskb[...]

    def over_z(relay_kind, final_kind, near_kind, far_kind, part, relay, final, everything, rows_a, weights_a, rows_b, weights_b):
        def one(i):
            t = zz(i)
            part[t] = jnp.where(
                low_lanes,
                fold(rows_a[t], weights_a[...].reshape(1024, -1)),
                fold(rows_b[t], weights_b[...].reshape(1024, -1)),
            )

        def begin():
            @pl.loop(3, 6)
            def _(i):
                one(i)

            copy(relay_kind, part.at[zz(-3)], relay.at[0], 0, 0, on_z(-1)).start()
            copy(relay_kind, part.at[zz(3)], relay.at[1], 1, 1, on_z(1)).start()
            copy(relay_kind, part.at[zz(4)], relay.at[2], 2, 2, on_z(2 * side)).start()

        def begin_near():
            @pl.loop(0, 2)
            def _(j):
                one(1 + 6 * j)

            copy(final_kind, part.at[zz(1)], final.at[0], 0, 0, on_z(1)).start()
            copy(final_kind, part.at[zz(-1)], final.at[1], 1, 1, on_z(-1)).start()

        def begin_own():
            @pl.loop(0, 3)
            def _(j):
                one(j * (j + 1))

        def pass_on():
            for i in range(3):
                arrived(relay_kind, relay.at[i], i)
            part[zz(-2)] += relay[0]
            part[zz(2)] += relay[1]
            part[zz(2 * side)] += relay[2]
            copy(final_kind, part.at[zz(2)], final.at[2], 2, 2, on_z(2)).start()
            copy(final_kind, part.at[zz(-2)], final.at[3], 3, 3, on_z(-2)).start()

        def publish():
            for i in range(4):
                arrived(final_kind, final.at[i], i)
            total = part[z] + final[0] + final[1] + final[2] + final[3]
            everything[z] = total.astype(BF)
            for i, step in enumerate((1, -1, 2, -2)):
                copy(near_kind, everything.at[z], everything.at[z], i, i, on_z(step)).start()

        def forward():
            arrived(near_kind, everything.at[zz(-2)], 2)
            arrived(near_kind, everything.at[zz(2)], 3)
            for i, (chunk, step) in enumerate(((-2, 1), (2, -1), (2 * side, -2 * side))):
                copy(far_kind, everything.at[zz(chunk)], everything.at[zz(chunk)], i, i, on_z(step)).start()

        def collect():
            arrived(near_kind, everything.at[zz(-1)], 0)
            arrived(near_kind, everything.at[zz(1)], 1)
            arrived(far_kind, everything.at[zz(-3)], 0)
            arrived(far_kind, everything.at[zz(3)], 1)
            arrived(far_kind, everything.at[zz(4)], 2)

        def finish():
            left(relay_kind, part.at[zz(-3)], 0)
            left(relay_kind, part.at[zz(3)], 1)
            left(relay_kind, part.at[zz(4)], 2)
            left(final_kind, part.at[zz(1)], 0)
            left(final_kind, part.at[zz(-1)], 1)
            left(final_kind, part.at[zz(2)], 2)
            left(final_kind, part.at[zz(-2)], 3)
            for i in range(4):
                left(near_kind, everything.at[z], i)
            for i in range(3):
                left(far_kind, everything.at[z], i)

        return begin, pass_on, publish, forward, collect, finish, begin_near, begin_own

    back = over_z(B_RELAY, B_FINAL, B_NEAR, B_FAR, bpart, brelay, bfinal, ball, rga, ua, rgb, ub)
    low = over_z(L_RELAY, L_FINAL, L_NEAR, L_FAR, lpart, lrelay, lfinal, lall, rxa, da, rxb, db)

    route_x(0, 2, hold=True)
    g_step(1)
    opposite_ring(FU_A, ua, x)
    opposite_ring(FU_B, ub, y)

    @pl.loop(1, 8)
    def _(d):
        fa = (m_a + d) % 8
        fb = (m_b + d) % 8
        arrived(G_A, rga.at[fa], fa)
        arrived(G_B, rgb.at[fb], fb)

    spread_ring(D_A, D_B, d_ref.at[:, pl.ds(0, HALF)], d_ref.at[:, pl.ds(HALF, HALF)], da, db)
    release_x(0, 2)
    back[0]()
    back[6]()
    back[7]()
    route_x(2, 4)
    back[1]()
    route_x(4, 6)
    back[2]()
    route_x(6, 8)
    back[3]()
    forward_ring(D_A, FD_A, da, x, ring_x)
    forward_ring(D_B, FD_B, db, y, ring_y)
    back[4]()
    opposite_ring(FD_A, da, x)
    opposite_ring(FD_B, db, y)

    def give_back(x_kind, kind, m, on, masked, is_a, weights, out, ret, d):
        s = (m + d) % 8
        block = spread(ball[s], is_a)
        masked[s] = block
        value = (
            adapter_scale * jnp.dot(block, weights[...].reshape(1024, HALF), preferred_element_type=F32)
        ).astype(BF)

        @pl.when(d != 0)
        def _():
            left(x_kind, out.at[s], s)
            out[s] = value
            copy(kind, out.at[s], ret.at[m], s, m, on(s)).start()

        @pl.when(d == 0)
        def _():
            ret[m] = value

    def give_back_all(lo, hi):
        with jax.named_scope("give_back"):

            @pl.loop(lo, hi)
            def _(k):
                d = near_first(k)
                give_back(X_A, R_A, m_a, on_a, ma, True, da, sxa, reta, d)
                give_back(X_B, R_B, m_b, on_b, mb, False, db, sxb, retb, d)

    give_back_all(0, 2)

    with jax.named_scope("wait_x"):

        @pl.loop(1, 8)
        def _(d):
            fa = (m_a + d) % 8
            fb = (m_b + d) % 8
            arrived(X_A, rxa.at[fa], fa)
            arrived(X_B, rxb.at[fb], fb)

    low[0]()
    give_back_all(2, 4)
    low[6]()
    low[7]()
    give_back_all(4, 6)
    low[1]()
    give_back_all(6, 8)

    def gradient(masked, rows, q):
        return adapter_scale * lax.dot_general(
            masked[:, :, pl.ds(pl.multiple_of(q * OWN, OWN), OWN)].reshape(8 * SLOTS, OWN),
            rows[...].reshape(8 * SLOTS, -1),
            (((0,), (0,)), ((), ())),
            preferred_element_type=F32,
        )

    def to_owners(kind, m, ring, masked, rows, part, recv, own, half, first):
        across, after, before = (m + 2) % 4, (m + 1) % 4, (m + 3) % 4
        if first:
            part[across] = gradient(masked, rows, across).astype(part.dtype)
            copy(kind, upper(part, across), upper(recv, 2), 2, 2, ring(after)).start()
            copy(kind, lower(part, across), lower(recv, 2), 3, 3, ring(before)).start()
            own[half] = gradient(masked, rows, m)
        else:
            for t, slot, edge, at in ((after, 0, upper, 0), (before, 1, lower, OWN // 2)):
                value = gradient(masked, rows, t)
                arrived(kind, edge(recv, 2), 2 + slot)
                part[t] = value.astype(part.dtype)
                rows_of = pl.ds(at, OWN // 2)
                part[t, rows_of, :] = (
                    value[at : at + OWN // 2] + recv[2, rows_of, :].astype(F32)
                ).astype(part.dtype)
                copy(kind, part.at[t], recv.at[slot], slot, slot, ring(t)).start()

    def from_neighbours(kind, recv, own, half):
        for slot in range(2):
            arrived(kind, recv.at[slot], slot)
        own[half] += recv[0].astype(F32) + recv[1].astype(F32)

    def sent_to_owners(kind, m, part):
        across = (m + 2) % 4
        left(kind, part.at[0], 0)
        left(kind, part.at[0], 1)
        left(kind, upper(part, across), 2)
        left(kind, lower(part, across), 3)

    def down_gradient(first):
        with jax.named_scope("down_gradient"):
            to_owners(DG_A, x, ring_x, ma, rxa, dga, dgra, dgo, 0, first)
            to_owners(DG_B, y, ring_y, mb, rxb, dgb, dgrb, dgo, 1, first)

    down_gradient(True)
    low[2]()

    def frozen():
        with jax.named_scope("frozen"):
            arrived(GR, g_half(-4, 0), 4)
            arrived(GL, g_half(4, 1), 4)
            w_in.wait()

            @pl.loop(0, ROWS // TILE)
            def _(i):
                rows = pl.ds(pl.multiple_of(i * TILE, TILE), TILE)
                acc[rows, :] += lax.dot_general(
                    gfull[rows, :], wv[...], (((1,), (1,)), ((), ())), preferred_element_type=F32
                )

    lanes = lax.broadcasted_iota(jnp.int32, (TILE, SLOTS), 1)

    def take(pair_number, last=False):
        with jax.named_scope("take_back"):
            blocks = []
            for j in range(2):
                d = near_first(jnp.int32(2 * pair_number + j))
                ta = (m_a - d + 8) % 8
                tb = (m_b - d + 8) % 8

                @pl.when(d != 0)
                def _():
                    arrived(R_A, reta.at[ta], ta)
                    arrived(R_B, retb.at[tb], tb)

                blocks.append((ta, tb))

            @pl.loop(0, ROWS // TILE)
            def _(i):
                rows = pl.ds(pl.multiple_of(i * TILE, TILE), TILE)
                slots = cols[rows, :].astype(jnp.int32)
                for half, ret in enumerate((reta, retb)):
                    here = pl.ds(half * HALF, HALF)
                    total = acc[rows, here] if pair_number else jnp.zeros((TILE, HALF), F32)
                    for ts in blocks:
                        t = ts[half]
                        pick = jnp.where(lanes + t * SLOTS == slots[:, half : half + 1], 1.0, 0.0).astype(BF)
                        total = total + jnp.dot(pick, ret[t], preferred_element_type=F32)
                    if last:
                        xv[rows, here] = total.astype(BF)
                    else:
                        acc[rows, here] = total
                if last:
                    pltpu.make_async_copy(xv.at[rows, :], out_hbm.at[rows, :], loc.at[2 + i]).start()

    def to_owner(kind, m, ring, masked, rows, part, recv, own, half, d):
        q = (m + d) % 4
        value = gradient(masked, rows, q)

        @pl.when(d == 4)
        def _():
            own[half] = value

        @pl.when(d != 4)
        def _():
            part[q] = value
            copy(kind, part.at[q], recv.at[m], q, m, ring(q)).start()

    take(0)
    low[3]()
    g_step(2)
    take(1)
    down_gradient(False)
    low[4]()

    with jax.named_scope("up_gradient"):

        @pl.loop(0, 8)
        def _(s):
            ma[s] = spread(lall[s], True)
            mb[s] = spread(lall[s], False)

        @pl.loop(1, 5)
        def _(d):
            to_owner(UG_A, x, ring_x, ma, rga, uga, ugra, ugo, 0, d)
            to_owner(UG_B, y, ring_y, mb, rgb, ugb, ugrb, ugo, 1, d)

    g_step(3)
    take(2)
    frozen()
    take(3, True)

    with jax.named_scope("down_sum"):
        from_neighbours(DG_A, dgra, dgo, 0)
        from_neighbours(DG_B, dgrb, dgo, 1)
        down_ref[:, :HALF] = dgo[0]
        down_ref[:, HALF:] = dgo[1]

    with jax.named_scope("up_sum"):

        @pl.loop(1, 4)
        def _(d):
            fx = (x + d) % 4
            fy = (y + d) % 4
            arrived(UG_A, ugra.at[fx], fx)
            arrived(UG_B, ugrb.at[fy], fy)
            ugo[0] += ugra[fx]
            ugo[1] += ugrb[fy]

        up_ref[...] = ugo[0] + ugo[1]

    @pl.loop(1, 8)
    def _(d):
        ta = (m_a + d) % 8
        tb = (m_b + d) % 8
        left(G_A, sga.at[ta], ta)
        left(G_B, sgb.at[tb], tb)
        left(R_A, sxa.at[ta], ta)
        left(R_B, sxb.at[tb], tb)

    for d in (1, 3):
        tx = (x + d) % 4
        ty = (y + d) % 4
        left(U_A, u_ref, tx)
        left(U_B, u_ref, ty)
        left(D_A, d_ref.at[:, pl.ds(0, HALF)], tx)
        left(D_B, d_ref.at[:, pl.ds(HALF, HALF)], ty)
    for i in range(2):
        left(FU_A, upper(ua, 0), i)
        left(FU_B, upper(ub, 0), i)
        left(FD_A, upper(da, 0), i)
        left(FD_B, upper(db, 0), i)
    sent_to_owners(DG_A, x, dga)
    sent_to_owners(DG_B, y, dgb)

    @pl.loop(1, 4)
    def _(d):
        left(UG_A, uga.at[(x + d) % 4], (x + d) % 4)
        left(UG_B, ugb.at[(y + d) % 4], (y + d) % 4)


    back[5]()
    low[5]()
    left(GR, g_ref, 0)
    left(GL, g_ref, 0)
    for i in (1, 2):
        left(GR, g_whole(-i), i)
        left(GL, g_whole(i), i)
    left(GR, g_half(-3, 0), 3)
    left(GL, g_half(3, 1), 3)

    @pl.loop(0, ROWS // TILE)
    def _(i):
        rows = pl.ds(pl.multiple_of(i * TILE, TILE), TILE)
        pltpu.make_async_copy(xv.at[rows, :], out_hbm.at[rows, :], loc.at[2 + i]).wait()


def adapter_backward(ids, x, g, w, d, u):
    vmem = pl.BlockSpec(memory_space=pltpu.VMEM)
    hbm = pl.BlockSpec(memory_space=pl.ANY)

    def blocks(count, width, dtype=BF):
        return pltpu.VMEM((count, SLOTS, width), dtype)

    def chunk(width, dtype=BF):
        return pltpu.VMEM((4, OWN, width), dtype)

    sums = [blocks(8, 128, F32), blocks(3, 128, F32), blocks(4, 128, F32), blocks(8, 128)]
    return pl.pallas_call(
        adapter_kernel,
        out_shape=(
            jax.ShapeDtypeStruct((ROWS, 2 * HALF), BF),
            jax.ShapeDtypeStruct((OWN, 2 * HALF), F32),
            jax.ShapeDtypeStruct((OWN, GW), F32),
        ),
        in_specs=[vmem, hbm, vmem, hbm, vmem, vmem],
        out_specs=(hbm, vmem, vmem),
        scratch_shapes=[
            pltpu.VMEM((ROWS, 2 * HALF), BF), pltpu.VMEM((2 * HALF, 1024), BF),
            pltpu.VMEM((1, ROWS), jnp.int32), pltpu.VMEM((1, ROWS), jnp.int32), pltpu.VMEM((ROWS, 8), F32),
            blocks(8, HALF), blocks(8, HALF), blocks(8, GW), blocks(8, GW),
            blocks(8, HALF), blocks(8, HALF), blocks(8, GW), blocks(8, GW),
            chunk(HALF), chunk(HALF), chunk(GW), chunk(GW), pltpu.VMEM((SLOTS, 1024), BF),
            *sums, *sums,
            blocks(8, 1024), blocks(8, 1024), blocks(8, HALF), blocks(8, HALF),
            chunk(HALF), chunk(HALF), chunk(HALF), chunk(HALF), pltpu.VMEM((2, OWN, HALF), F32),
            chunk(GW, F32), chunk(GW, F32), chunk(GW, F32), chunk(GW, F32), pltpu.VMEM((2, OWN, GW), F32),
            pltpu.VMEM((ROWS, 1024), BF), pltpu.VMEM((ROWS, 2 * HALF), F32),
            pltpu.SemaphoreType.DMA((28, 8)), pltpu.SemaphoreType.DMA((28, 8)), pltpu.SemaphoreType.DMA((8,)),
        ],
        compiler_params=pltpu.CompilerParams(
            collective_id=0, has_side_effects=True, vmem_limit_bytes=62 * 2**20
        ),
        cost_estimate=pl.CostEstimate(flops=32 * 10**9, bytes_accessed=12 * 10**6, transcendentals=0),
        name="adapter_backward",
    )(ids, x, g, w, d, u)


def body(
    activations,
    output_gradient,
    adapter_of_row,
    frozen_value_weight,
    adapter_down_weight,
    adapter_up_weight,
):
    input_gradient, down, up = adapter_backward(
        adapter_of_row.reshape(1, ROWS),
        activations,
        output_gradient,
        frozen_value_weight,
        adapter_down_weight.reshape(OWN, 2 * HALF),
        adapter_up_weight.reshape(OWN, GW),
    )
    return input_gradient, down.reshape(4, RANK, 2 * HALF), up.reshape(4, RANK, GW)


def solution(mesh):
    in_specs = (
        P("adapter", "tensor"),
        P("adapter", "tensor"),
        P("adapter", None),
        P("tensor", None),
        P("adapter", None, "tensor"),
        P("adapter", None, "tensor"),
    )
    out_specs = (P("adapter", "tensor"), P("adapter", None, "tensor"), P("adapter", None, "tensor"))
    return jax.shard_map(body, mesh=mesh, in_specs=in_specs, out_specs=out_specs, check_vma=False)
```

```python
import jax
import jax.numpy as jnp
from jax import lax
from jax.experimental import pallas as pl
from jax.experimental.pallas import tpu as pltpu
from jax.sharding import PartitionSpec as P

adapter_scale = 2.0
MESH = pl.DeviceIdType.MESH
BF = jnp.bfloat16
F32 = jnp.float32

MOST = 15
SLOTS = 240
HALF = 512
ROWS = 1536
RANK = 64
GW = 128
OWN = 256
TILE = 256

(U_A, U_B, G_A, G_B, D_A, D_B, X_A, X_B, R_A, R_B, DG_A, DG_B, UG_A, UG_B, GR, GL,
 B_RELAY, B_FINAL, B_NEAR, B_FAR, L_RELAY, L_FINAL, L_NEAR, L_FAR, FU_A, FU_B, FD_A, FD_B) = range(28)


def adapter_kernel(
    ids_ref, x_hbm, g_ref, w_hbm, d_ref, u_ref,
    out_hbm, down_ref, up_ref,
    xv, wv, sa_ref, sb_ref, cols,
    sxa, sxb, sga, sgb, rxa, rxb, rga, rgb,
    da, db, ua, ub, maskb,
    bpart, brelay, bfinal, ball, lpart, lrelay, lfinal, lall,
    ma, mb, reta, retb,
    dga, dgb, dgra, dgrb, dgo, uga, ugb, ugra, ugrb, ugo,
    gfull, acc,
    ss, rs, loc,
):
    a = lax.axis_index("adapter")
    z = lax.axis_index("tensor")
    c = a % 2
    y = (a // 2) % 4
    x = a // 8
    m_a = y * 2 + c
    m_b = x * 2 + c
    side = 2 * (z % 2) - 1

    def on_a(t):
        return ((x * 4 + t // 2) * 2 + t % 2, z)

    def on_b(t):
        return (((t // 2) * 4 + y) * 2 + t % 2, z)

    def ring_x(t):
        return ((t * 4 + y) * 2 + c, z)

    def ring_y(t):
        return ((x * 4 + t) * 2 + c, z)

    def zz(i):
        return (z + i + 16) % 8

    def on_z(i):
        return (a, zz(i))

    def copy(kind, src, dst, to, me, device):
        return pltpu.make_async_remote_copy(
            src_ref=src, dst_ref=dst, send_sem=ss.at[kind, to], recv_sem=rs.at[kind, me],
            device_id=device, device_id_type=MESH,
        )

    def arrived(kind, dst, frm):
        copy(kind, dst, dst, frm, frm, (a, z)).wait_recv()

    def left(kind, src, to):
        copy(kind, src, src, to, to, (a, z)).wait_send()

    def near_first(k):
        return jnp.where(k < 4, 2 + 4 * (k % 2) + k // 2, 4 * (1 - (k - 4) // 2) + k % 2)

    x_in = pltpu.make_async_copy(x_hbm, xv, loc.at[0])
    x_in.start()
    w_in = pltpu.make_async_copy(w_hbm, wv, loc.at[1])
    w_in.start()

    barrier = pltpu.get_barrier_semaphore()

    @pl.loop(1, 8)
    def _(d):
        pl.semaphore_signal(barrier, inc=1, device_id=on_a((m_a + d) % 8), device_id_type=MESH)
        pl.semaphore_signal(barrier, inc=1, device_id=on_z(d), device_id_type=MESH)

    @pl.loop(2, 8)
    def _(d):
        t = ((x * 2) + d) % 8
        pl.semaphore_signal(barrier, inc=1, device_id=on_b(t), device_id_type=MESH)

    with jax.named_scope("slots"):
        ids = ids_ref[...]
        hot = jnp.where(lax.broadcasted_iota(jnp.int32, (128, ROWS), 0) == ids, 1.0, 0.0)
        before = jnp.where(
            lax.broadcasted_iota(jnp.int32, (TILE, TILE), 0) < lax.broadcasted_iota(jnp.int32, (TILE, TILE), 1), 1.0, 0.0
        ).astype(BF)
        seen = jnp.zeros((128, 1), F32)
        places = []
        for q in range(ROWS // TILE):
            part = hot[:, q * TILE : (q + 1) * TILE]
            count = jnp.dot(part.astype(BF), before, preferred_element_type=F32) + seen
            places.append(jnp.sum(count * part, axis=0, keepdims=True))
            seen = seen + jnp.sum(part, axis=1, keepdims=True)
        place = jnp.concatenate(places, axis=1).astype(jnp.int32)
        owner, within = ids >> 2, ids & 3
        core, oy, ox = owner & 1, (owner >> 1) & 3, owner >> 3
        slot_a = (oy * 2 + core) * SLOTS + (ox * 4 + within) * MOST + place
        slot_b = (ox * 2 + core) * SLOTS + (oy * 4 + within) * MOST + place
        sa_ref[...] = slot_a
        sb_ref[...] = slot_b
        cols[...] = jnp.concatenate([slot_a.astype(F32), slot_b.astype(F32)] * 4, axis=0).T

        first = (lax.broadcasted_iota(jnp.int32, (SLOTS, 1024), 1) >> 6) * MOST
        row = lax.broadcasted_iota(jnp.int32, (SLOTS, 1024), 0)
        maskb[...] = jnp.where((row >= first) & (row < first + MOST), 1.0, 0.0).astype(BF)

    pl.semaphore_wait(barrier, 20)

    def spread_ring(kind_a, kind_b, src_a, src_b, dst_a, dst_b):
        for d in (1, 3):
            tx = (x + d) % 4
            ty = (y + d) % 4
            copy(kind_a, src_a, dst_a.at[x], tx, x, ring_x(tx)).start()
            copy(kind_b, src_b, dst_b.at[y], ty, y, ring_y(ty)).start()

    def upper(ref, t):
        return ref.at[t, pl.ds(0, OWN // 2), :]

    def lower(ref, t):
        return ref.at[t, pl.ds(OWN // 2, OWN // 2), :]

    def forward_ring(kind, far_kind, dst, m, ring):
        before, after = (m + 3) % 4, (m + 1) % 4
        arrived(kind, dst.at[before], before)
        arrived(kind, dst.at[after], after)
        copy(far_kind, upper(dst, before), upper(dst, before), 0, 0, ring(after)).start()
        copy(far_kind, lower(dst, after), lower(dst, after), 1, 1, ring(before)).start()

    def opposite_ring(far_kind, dst, m):
        across = (m + 2) % 4
        arrived(far_kind, upper(dst, across), 0)
        arrived(far_kind, lower(dst, across), 1)

    spread_ring(U_A, U_B, u_ref, u_ref, ua, ub)
    ua[x] = u_ref[...]
    ub[y] = u_ref[...]

    def g_cols(i):
        return pl.ds(pl.multiple_of(zz(i) * GW, GW), GW)

    def g_whole(i):
        return gfull.at[:, g_cols(i)]

    def g_half(i, upper):
        return gfull.at[pl.ds(upper * (ROWS // 2), ROWS // 2), g_cols(i)]

    copy(GR, g_ref, g_whole(0), 0, 1, on_z(1)).start()
    copy(GL, g_ref, g_whole(0), 0, 1, on_z(-1)).start()

    def g_step(i):
        arrived(GR, g_whole(-i), i)
        arrived(GL, g_whole(i), i)
        if i < 3:
            copy(GR, g_whole(-i), g_whole(-i), i, i + 1, on_z(1)).start()
            copy(GL, g_whole(i), g_whole(i), i, i + 1, on_z(-1)).start()
        else:
            copy(GR, g_half(-i, 0), g_half(-i, 0), i, i + 1, on_z(1)).start()
            copy(GL, g_half(i, 1), g_half(i, 1), i, i + 1, on_z(-1)).start()

    slot_rows = lax.broadcasted_iota(jnp.int32, (SLOTS, ROWS), 0)

    def choose(s_ref, t):
        return jnp.where(slot_rows + t * SLOTS == s_ref[...], 1.0, 0.0).astype(BF)

    def route(kind, m, on, s_ref, value, send, recv, d, hold=False):
        t = (m + d) % 8
        block = jnp.dot(choose(s_ref, t), value, preferred_element_type=F32).astype(BF)

        @pl.when(d == 0)
        def _():
            recv[m] = block

        @pl.when(d != 0)
        def _():
            send[t] = block
            if not hold:
                copy(kind, send.at[t], recv.at[m], t, m, on(t)).start()

    with jax.named_scope("route_g"):

        @pl.loop(0, 8)
        def _(k):
            d = near_first(k)
            route(G_A, m_a, on_a, sa_ref, g_ref[...], sga, rga, d)
            route(G_B, m_b, on_b, sb_ref, g_ref[...], sgb, rgb, d)

    gfull[:, g_cols(0)] = g_ref[...]

    spread_ring(D_A, D_B, d_ref.at[:, pl.ds(0, HALF)], d_ref.at[:, pl.ds(HALF, HALF)], da, db)
    forward_ring(U_A, FU_A, ua, x, ring_x)
    forward_ring(U_B, FU_B, ub, y, ring_y)
    da[x] = d_ref[:, :HALF]
    db[y] = d_ref[:, HALF:]
    x_in.wait()

    def route_x(lo, hi, hold=False):
        with jax.named_scope("route_x"):

            @pl.loop(lo, hi)
            def _(k):
                d = near_first(k)
                route(X_A, m_a, on_a, sa_ref, xv[:, :HALF], sxa, rxa, d, hold)
                route(X_B, m_b, on_b, sb_ref, xv[:, HALF:], sxb, rxb, d, hold)

    def release_x(lo, hi):
        @pl.loop(lo, hi)
        def _(k):
            d = near_first(k)
            ta = (m_a + d) % 8
            tb = (m_b + d) % 8
            copy(X_A, sxa.at[ta], rxa.at[m_a], ta, m_a, on_a(ta)).start()
            copy(X_B, sxb.at[tb], rxb.at[m_b], tb, m_b, on_b(tb)).start()

    low_lanes = lax.broadcasted_iota(jnp.int32, (SLOTS, 128), 1) < RANK

    def fold(rows, weights):
        product = lax.dot_general(rows, weights, (((1,), (1,)), ((), ())), preferred_element_type=F32)
        product = product * maskb[...].astype(F32)
        total = product[:, :128]
        for i in range(1, 8):
            total = total + product[:, i * 128 : (i + 1) * 128]
        return total + pltpu.roll(total, RANK, 1)

    def spread(both, is_a):
        wide = both.astype(F32)
        turned = pltpu.roll(wide, RANK, 1)
        one = (jnp.where(low_lanes, wide, turned) if is_a else jnp.where(low_lanes, turned, wide)).astype(BF)
        return jnp.concatenate([one] * 8, axis=1) * maskb[...]

    def over_z(relay_kind, final_kind, near_kind, far_kind, part, relay, final, everything, rows_a, weights_a, rows_b, weights_b):
        def one(i):
            t = zz(i)
            part[t] = jnp.where(
                low_lanes,
                fold(rows_a[t], weights_a[...].reshape(1024, -1)),
                fold(rows_b[t], weights_b[...].reshape(1024, -1)),
            )

        def begin():
            @pl.loop(3, 6)
            def _(i):
                one(i)

            copy(relay_kind, part.at[zz(-3)], relay.at[0], 0, 0, on_z(-1)).start()
            copy(relay_kind, part.at[zz(3)], relay.at[1], 1, 1, on_z(1)).start()
            copy(relay_kind, part.at[zz(4)], relay.at[2], 2, 2, on_z(2 * side)).start()

        def begin_near():
            @pl.loop(0, 2)
            def _(j):
                one(1 + 6 * j)

            copy(final_kind, part.at[zz(1)], final.at[0], 0, 0, on_z(1)).start()
            copy(final_kind, part.at[zz(-1)], final.at[1], 1, 1, on_z(-1)).start()

        def begin_own():
            @pl.loop(0, 3)
            def _(j):
                one(j * (j + 1))

        def pass_on():
            for i in range(3):
                arrived(relay_kind, relay.at[i], i)
            part[zz(-2)] += relay[0]
            part[zz(2)] += relay[1]
            part[zz(2 * side)] += relay[2]
            copy(final_kind, part.at[zz(2)], final.at[2], 2, 2, on_z(2)).start()
            copy(final_kind, part.at[zz(-2)], final.at[3], 3, 3, on_z(-2)).start()

        def publish():
            for i in range(4):
                arrived(final_kind, final.at[i], i)
            total = part[z] + final[0] + final[1] + final[2] + final[3]
            everything[z] = total.astype(BF)
            for i, step in enumerate((1, -1, 2, -2)):
                copy(near_kind, everything.at[z], everything.at[z], i, i, on_z(step)).start()

        def forward():
            arrived(near_kind, everything.at[zz(-2)], 2)
            arrived(near_kind, everything.at[zz(2)], 3)
            for i, (chunk, step) in enumerate(((-2, 1), (2, -1), (2 * side, -2 * side))):
                copy(far_kind, everything.at[zz(chunk)], everything.at[zz(chunk)], i, i, on_z(step)).start()

        def collect():
            arrived(near_kind, everything.at[zz(-1)], 0)
            arrived(near_kind, everything.at[zz(1)], 1)
            arrived(far_kind, everything.at[zz(-3)], 0)
            arrived(far_kind, everything.at[zz(3)], 1)
            arrived(far_kind, everything.at[zz(4)], 2)

        def finish():
            left(relay_kind, part.at[zz(-3)], 0)
            left(relay_kind, part.at[zz(3)], 1)
            left(relay_kind, part.at[zz(4)], 2)
            left(final_kind, part.at[zz(1)], 0)
            left(final_kind, part.at[zz(-1)], 1)
            left(final_kind, part.at[zz(2)], 2)
            left(final_kind, part.at[zz(-2)], 3)
            for i in range(4):
                left(near_kind, everything.at[z], i)
            for i in range(3):
                left(far_kind, everything.at[z], i)

        return begin, pass_on, publish, forward, collect, finish, begin_near, begin_own

    back = over_z(B_RELAY, B_FINAL, B_NEAR, B_FAR, bpart, brelay, bfinal, ball, rga, ua, rgb, ub)
    low = over_z(L_RELAY, L_FINAL, L_NEAR, L_FAR, lpart, lrelay, lfinal, lall, rxa, da, rxb, db)

    route_x(0, 2, hold=True)
    g_step(1)
    opposite_ring(FU_A, ua, x)
    opposite_ring(FU_B, ub, y)

    @pl.loop(1, 8)
    def _(d):
        fa = (m_a + d) % 8
        fb = (m_b + d) % 8
        arrived(G_A, rga.at[fa], fa)
        arrived(G_B, rgb.at[fb], fb)

    release_x(0, 2)
    back[0]()
    back[6]()
    back[7]()
    route_x(2, 4)
    back[1]()
    route_x(4, 6)
    back[2]()
    route_x(6, 8)
    back[3]()
    forward_ring(D_A, FD_A, da, x, ring_x)
    forward_ring(D_B, FD_B, db, y, ring_y)
    back[4]()
    opposite_ring(FD_A, da, x)
    opposite_ring(FD_B, db, y)

    def give_back(x_kind, kind, m, on, masked, is_a, weights, out, ret, d):
        s = (m + d) % 8
        block = spread(ball[s], is_a)
        masked[s] = block
        value = (
            adapter_scale * jnp.dot(block, weights[...].reshape(1024, HALF), preferred_element_type=F32)
        ).astype(BF)

        @pl.when(d != 0)
        def _():
            left(x_kind, out.at[s], s)
            out[s] = value
            copy(kind, out.at[s], ret.at[m], s, m, on(s)).start()

        @pl.when(d == 0)
        def _():
            ret[m] = value

    def give_back_all(lo, hi):
        with jax.named_scope("give_back"):

            @pl.loop(lo, hi)
            def _(k):
                d = near_first(k)
                give_back(X_A, R_A, m_a, on_a, ma, True, da, sxa, reta, d)
                give_back(X_B, R_B, m_b, on_b, mb, False, db, sxb, retb, d)

    give_back_all(0, 2)

    with jax.named_scope("wait_x"):

        @pl.loop(1, 8)
        def _(d):
            fa = (m_a + d) % 8
            fb = (m_b + d) % 8
            arrived(X_A, rxa.at[fa], fa)
            arrived(X_B, rxb.at[fb], fb)

    low[0]()
    give_back_all(2, 4)
    low[6]()
    low[7]()
    low[1]()
    give_back_all(4, 8)

    def gradient(masked, rows, q):
        window = pl.ds(pl.multiple_of((q * 7) // 2 * 16, 16), 80)
        return adapter_scale * lax.dot_general(
            masked[:, window, pl.ds(pl.multiple_of(q * OWN, OWN), OWN)].reshape(8 * 80, OWN),
            rows[:, window, :].reshape(8 * 80, -1),
            (((0,), (0,)), ((), ())),
            preferred_element_type=F32,
        )

    def to_owners(kind, m, ring, masked, rows, part, recv, own, half, first):
        across, after, before = (m + 2) % 4, (m + 1) % 4, (m + 3) % 4
        if first:
            part[across] = gradient(masked, rows, across).astype(part.dtype)
            copy(kind, upper(part, across), upper(recv, 2), 2, 2, ring(after)).start()
            copy(kind, lower(part, across), lower(recv, 2), 3, 3, ring(before)).start()
            own[half] = gradient(masked, rows, m)
        else:
            for t, slot, edge, at in ((after, 0, upper, 0), (before, 1, lower, OWN // 2)):
                value = gradient(masked, rows, t)
                arrived(kind, edge(recv, 2), 2 + slot)
                part[t] = value.astype(part.dtype)
                rows_of = pl.ds(at, OWN // 2)
                part[t, rows_of, :] = (
                    value[at : at + OWN // 2] + recv[2, rows_of, :].astype(F32)
                ).astype(part.dtype)
                copy(kind, part.at[t], recv.at[slot], slot, slot, ring(t)).start()

    def from_neighbours(kind, recv, own, half):
        for slot in range(2):
            arrived(kind, recv.at[slot], slot)
        own[half] += recv[0].astype(F32) + recv[1].astype(F32)

    def sent_to_owners(kind, m, part):
        across = (m + 2) % 4
        left(kind, part.at[0], 0)
        left(kind, part.at[0], 1)
        left(kind, upper(part, across), 2)
        left(kind, lower(part, across), 3)

    def down_gradient(first):
        with jax.named_scope("down_gradient"):
            to_owners(DG_A, x, ring_x, ma, rxa, dga, dgra, dgo, 0, first)
            to_owners(DG_B, y, ring_y, mb, rxb, dgb, dgrb, dgo, 1, first)

    low[2]()
    down_gradient(True)

    def frozen():
        with jax.named_scope("frozen"):
            arrived(GR, g_half(-4, 0), 4)
            arrived(GL, g_half(4, 1), 4)
            w_in.wait()

            @pl.loop(0, ROWS // TILE)
            def _(i):
                rows = pl.ds(pl.multiple_of(i * TILE, TILE), TILE)
                acc[rows, :] += lax.dot_general(
                    gfull[rows, :], wv[...], (((1,), (1,)), ((), ())), preferred_element_type=F32
                )

    lanes = lax.broadcasted_iota(jnp.int32, (TILE, SLOTS), 1)

    def take(pair_number, last=False):
        with jax.named_scope("take_back"):
            blocks = []
            for j in range(2):
                d = near_first(jnp.int32(2 * pair_number + j))
                ta = (m_a - d + 8) % 8
                tb = (m_b - d + 8) % 8

                @pl.when(d != 0)
                def _():
                    arrived(R_A, reta.at[ta], ta)
                    arrived(R_B, retb.at[tb], tb)

                blocks.append((ta, tb))

            @pl.loop(0, ROWS // TILE)
            def _(i):
                rows = pl.ds(pl.multiple_of(i * TILE, TILE), TILE)
                slots = cols[rows, :].astype(jnp.int32)
                for half, ret in enumerate((reta, retb)):
                    here = pl.ds(half * HALF, HALF)
                    total = acc[rows, here] if pair_number else jnp.zeros((TILE, HALF), F32)
                    for ts in blocks:
                        t = ts[half]
                        pick = jnp.where(lanes + t * SLOTS == slots[:, half : half + 1], 1.0, 0.0).astype(BF)
                        total = total + jnp.dot(pick, ret[t], preferred_element_type=F32)
                    if last:
                        xv[rows, here] = total.astype(BF)
                    else:
                        acc[rows, here] = total
                if last:
                    pltpu.make_async_copy(xv.at[rows, :], out_hbm.at[rows, :], loc.at[2 + i]).start()

    def to_owner(kind, m, ring, masked, rows, part, recv, own, half, d):
        q = (m + d) % 4
        value = gradient(masked, rows, q)

        @pl.when(d == 4)
        def _():
            own[half] = value

        @pl.when(d != 4)
        def _():
            part[q] = value
            copy(kind, part.at[q], recv.at[m], q, m, ring(q)).start()

    low[3]()
    g_step(2)
    take(0)
    take(1)
    down_gradient(False)
    low[4]()

    with jax.named_scope("up_gradient"):

        @pl.loop(0, 8)
        def _(s):
            ma[s] = spread(lall[s], True)
            mb[s] = spread(lall[s], False)

        @pl.loop(1, 5)
        def _(d):
            to_owner(UG_A, x, ring_x, ma, rga, uga, ugra, ugo, 0, d)
            to_owner(UG_B, y, ring_y, mb, rgb, ugb, ugrb, ugo, 1, d)

    g_step(3)
    take(2)
    frozen()
    take(3, True)

    with jax.named_scope("down_sum"):
        from_neighbours(DG_A, dgra, dgo, 0)
        from_neighbours(DG_B, dgrb, dgo, 1)
        down_ref[:, :HALF] = dgo[0]
        down_ref[:, HALF:] = dgo[1]

    with jax.named_scope("up_sum"):

        @pl.loop(1, 4)
        def _(d):
            fx = (x + d) % 4
            fy = (y + d) % 4
            arrived(UG_A, ugra.at[fx], fx)
            arrived(UG_B, ugrb.at[fy], fy)
            ugo[0] += ugra[fx]
            ugo[1] += ugrb[fy]

        up_ref[...] = ugo[0] + ugo[1]

    @pl.loop(1, 8)
    def _(d):
        ta = (m_a + d) % 8
        tb = (m_b + d) % 8
        left(G_A, sga.at[ta], ta)
        left(G_B, sgb.at[tb], tb)
        left(R_A, sxa.at[ta], ta)
        left(R_B, sxb.at[tb], tb)

    for d in (1, 3):
        tx = (x + d) % 4
        ty = (y + d) % 4
        left(U_A, u_ref, tx)
        left(U_B, u_ref, ty)
        left(D_A, d_ref.at[:, pl.ds(0, HALF)], tx)
        left(D_B, d_ref.at[:, pl.ds(HALF, HALF)], ty)
    for i in range(2):
        left(FU_A, upper(ua, 0), i)
        left(FU_B, upper(ub, 0), i)
        left(FD_A, upper(da, 0), i)
        left(FD_B, upper(db, 0), i)
    sent_to_owners(DG_A, x, dga)
    sent_to_owners(DG_B, y, dgb)

    @pl.loop(1, 4)
    def _(d):
        left(UG_A, uga.at[(x + d) % 4], (x + d) % 4)
        left(UG_B, ugb.at[(y + d) % 4], (y + d) % 4)


    back[5]()
    low[5]()
    left(GR, g_ref, 0)
    left(GL, g_ref, 0)
    for i in (1, 2):
        left(GR, g_whole(-i), i)
        left(GL, g_whole(i), i)
    left(GR, g_half(-3, 0), 3)
    left(GL, g_half(3, 1), 3)

    @pl.loop(0, ROWS // TILE)
    def _(i):
        rows = pl.ds(pl.multiple_of(i * TILE, TILE), TILE)
        pltpu.make_async_copy(xv.at[rows, :], out_hbm.at[rows, :], loc.at[2 + i]).wait()


def adapter_backward(ids, x, g, w, d, u):
    vmem = pl.BlockSpec(memory_space=pltpu.VMEM)
    hbm = pl.BlockSpec(memory_space=pl.ANY)

    def blocks(count, width, dtype=BF):
        return pltpu.VMEM((count, SLOTS, width), dtype)

    def chunk(width, dtype=BF):
        return pltpu.VMEM((4, OWN, width), dtype)

    sums = [blocks(8, 128, F32), blocks(3, 128, F32), blocks(4, 128, F32), blocks(8, 128)]
    return pl.pallas_call(
        adapter_kernel,
        out_shape=(
            jax.ShapeDtypeStruct((ROWS, 2 * HALF), BF),
            jax.ShapeDtypeStruct((OWN, 2 * HALF), F32),
            jax.ShapeDtypeStruct((OWN, GW), F32),
        ),
        in_specs=[vmem, hbm, vmem, hbm, vmem, vmem],
        out_specs=(hbm, vmem, vmem),
        scratch_shapes=[
            pltpu.VMEM((ROWS, 2 * HALF), BF), pltpu.VMEM((2 * HALF, 1024), BF),
            pltpu.VMEM((1, ROWS), jnp.int32), pltpu.VMEM((1, ROWS), jnp.int32), pltpu.VMEM((ROWS, 8), F32),
            blocks(8, HALF), blocks(8, HALF), blocks(8, GW), blocks(8, GW),
            blocks(8, HALF), blocks(8, HALF), blocks(8, GW), blocks(8, GW),
            chunk(HALF), chunk(HALF), chunk(GW), chunk(GW), pltpu.VMEM((SLOTS, 1024), BF),
            *sums, *sums,
            blocks(8, 1024), blocks(8, 1024), blocks(8, HALF), blocks(8, HALF),
            chunk(HALF), chunk(HALF), chunk(HALF), chunk(HALF), pltpu.VMEM((2, OWN, HALF), F32),
            chunk(GW, F32), chunk(GW, F32), chunk(GW, F32), chunk(GW, F32), pltpu.VMEM((2, OWN, GW), F32),
            pltpu.VMEM((ROWS, 1024), BF), pltpu.VMEM((ROWS, 2 * HALF), F32),
            pltpu.SemaphoreType.DMA((28, 8)), pltpu.SemaphoreType.DMA((28, 8)), pltpu.SemaphoreType.DMA((8,)),
        ],
        compiler_params=pltpu.CompilerParams(
            collective_id=0, has_side_effects=True, vmem_limit_bytes=62 * 2**20
        ),
        cost_estimate=pl.CostEstimate(flops=32 * 10**9, bytes_accessed=12 * 10**6, transcendentals=0),
        name="adapter_backward",
    )(ids, x, g, w, d, u)


def body(
    activations,
    output_gradient,
    adapter_of_row,
    frozen_value_weight,
    adapter_down_weight,
    adapter_up_weight,
):
    input_gradient, down, up = adapter_backward(
        adapter_of_row.reshape(1, ROWS),
        activations,
        output_gradient,
        frozen_value_weight,
        adapter_down_weight.reshape(OWN, 2 * HALF),
        adapter_up_weight.reshape(OWN, GW),
    )
    return input_gradient, down.reshape(4, RANK, 2 * HALF), up.reshape(4, RANK, GW)


def solution(mesh):
    in_specs = (
        P("adapter", "tensor"),
        P("adapter", "tensor"),
        P("adapter", None),
        P("tensor", None),
        P("adapter", None, "tensor"),
        P("adapter", None, "tensor"),
    )
    out_specs = (P("adapter", "tensor"), P("adapter", None, "tensor"), P("adapter", None, "tensor"))
    return jax.shard_map(body, mesh=mesh, in_specs=in_specs, out_specs=out_specs, check_vma=False)
```
